32 devices in a mesh: groups: 2 (over x), loop: 16 (over z, y, core).
Axes of the slice: x: 2, y: 2, z: 4, core: 2. Of those that a mesh axis runs over, the one named last changes fastest.
Arguments:
- queries: bfloat16 [256, 4, 64, 128], P(('groups', 'loop')), parts along dimension 0, may hold values from -16 to 16
- new_keys: bfloat16 [256, 4, 4, 128], P(('groups', 'loop')), parts along dimension 0, may hold values from -8 to 8
- new_values: bfloat16 [256, 4, 4, 128], P(('groups', 'loop')), parts along dimension 0, may hold values from -12 to 12
- suffix_keys: bfloat16 [256, 256, 4, 128], P(('groups', 'loop')), parts along dimension 0, may hold values from -8 to 8
- suffix_values: bfloat16 [256, 256, 4, 128], P(('groups', 'loop')), parts along dimension 0, may hold values from -12 to 12
- suffix_len: int32 [256], P(('groups', 'loop')), parts along dimension 0, may hold values from 1 to 256, 16384 in all
- prefix_keys: bfloat16 [32, 64, 4, 128], P(('groups', 'loop')), parts along dimension 0, may hold values from -8 to 8
- prefix_values: bfloat16 [32, 64, 4, 128], P(('groups', 'loop')), parts along dimension 0, may hold values from -12 to 12
- block_ids: int32 [32], P(('groups', 'loop')), parts along dimension 0, may hold values from 0 to 15, each once
- block_lists: int32 [256, 4], P(('groups', 'loop')), parts along dimension 0, may hold values from 0 to 15, all different within a row
Outputs:
- attended: bfloat16 [256, 4, 64, 128], P(('groups', 'loop')), parts along dimension 0
The draws below stay inside these ranges and needn't reach their ends.
There are 2 independent parts, one for each index of `groups`. The reference program is written for one: setup_inputs(seed, part) draws one part's arguments, and reference() takes and returns one part's arrays. A program takes and returns all parts, laid end to end along the dimension named above; each array names one. Nothing has to cross between parts.
Inputs may be any that keep to these rules, and one draw needn't show every extreme that they name: `block_ids`: each slot holds a different block. `block_lists`: each request names 4 different blocks; every block is named by some request. `suffix_len`: some request uses all 256 slots.
All inputs are finite; a program needn't handle non-finite values. No bound on the sum of `suffix_len` on one device may be relied on, other than what follows from the above.
Results may differ from the reference program's by a relative error of at most 0.004.
Values may be sent and summed in bfloat16 or wider, within the bound.
A program may use at most 64 MiB of HBM per device.

```python
import math
import jax
import jax.numpy as jnp
import numpy as np
from jax import lax

SUF = 256
STEPS = 4
NBR = 4
BS = 64
HD = 128
QH = 64
KVH = 4
GROUP = 16
REQUESTS = 128
NBLK = 16


def joint_draw(key):
    folded = jax.random.fold_in(key, 17)
    key_query, key_fresh = jax.random.split(folded, 2)
    query_rows = jnp.clip(jax.random.normal(key_query, (REQUESTS, STEPS, QH, HD), jnp.float32), -6.0, 6.0)
    fresh_keys = jnp.clip(2.0 * jax.random.normal(key_fresh, (REQUESTS, STEPS, KVH, HD), jnp.float32), -8.0, 8.0)
    return (query_rows, fresh_keys)


def draw_queries(key, part):
    return joint_draw(key)[0].astype(jnp.bfloat16)


def draw_new_keys(key, part):
    return joint_draw(key)[1].astype(jnp.bfloat16)


def steps_of(stream_key, extent, cuts, least, top_value):
    level, own = 1.0, jax.random.fold_in(stream_key, 6)
    for dim, parts in cuts:
        steps = jnp.exp(jax.random.uniform(jax.random.fold_in(own, dim), (parts,), jnp.float32, least / len(cuts), top_value / len(cuts)))
        level = level * jnp.repeat(steps, extent[dim] // parts).reshape([-1 if axis == dim else 1 for axis in range(len(extent))])
    return level


def different_ones(rng, rows, number_of, top, lift):
    sequence = jax.random.permutation(jax.random.fold_in(rng, 1), number_of)
    favour = sequence
    for power in range(3):
        favour = favour * favour // number_of
    favour = favour * lift // number_of
    lots = jax.random.randint(jax.random.fold_in(rng, 2), (rows, number_of), 0, 4096) + favour
    holders = jax.random.permutation(jax.random.fold_in(rng, 3), rows)[jnp.arange(number_of) % rows]
    lots = jnp.where(jnp.arange(rows)[:, None] == holders[None, :], 1 << 14, lots)
    priority = lots * number_of + jnp.arange(number_of)
    return lax.top_k(priority.astype(jnp.int32), top)[1].astype(jnp.int32)


def length_profile(number_of, total, reach, slope):
    loads = [(1 << 20) // math.isqrt(standing ** slope) + 1 for standing in range(2, number_of + 1)]
    surplus, counts = total - reach - (number_of - 1), [1] * (number_of - 1)
    while surplus > 0:
        movable = [i for i in range(number_of - 1) if counts[i] < reach]
        pool, remaining = sum([loads[i] for i in movable]), surplus
        for i in movable:
            extra = min(reach - counts[i], max(1, remaining * loads[i] // pool), surplus)
            counts[i] = counts[i] + extra
            surplus = surplus - extra
    return np.array([reach] + counts)


def ragged_sizes(rng, number_of, total, bound, slope):
    if number_of == 2:
        one = jax.random.randint(rng, (), max(1, total - bound), min(bound, total - 1) + 1)
        return jnp.stack([one, total - one])
    tallies = jnp.asarray(length_profile(number_of, total, bound, slope), jnp.int32)
    twos = (number_of - 1) // 2
    source_of, sink = tallies[1:1 + 2 * twos:2], tallies[2:2 + 2 * twos:2]
    margin = jnp.minimum(source_of - 1, bound - sink)
    shifted = jax.random.randint(jax.random.fold_in(rng, 1), (twos,), 0, 1 << 20) % (margin + 1)
    tallies = tallies.at[1:1 + 2 * twos:2].set(source_of - shifted).at[2:2 + 2 * twos:2].set(sink + shifted)
    return tallies[jax.random.permutation(jax.random.fold_in(rng, 2), number_of)]


def scatter_about(rng, extent, scale, most, pieces=(), kind=jnp.bfloat16):
    result = scale * jax.random.normal(rng, extent, jnp.float32)
    if pieces:
        result = result * steps_of(rng, extent, pieces, -0.22, 0.18)
    return jnp.clip(result, -most, most).astype(kind)


def setup_inputs(seed: int = 0, part: int = 0) -> dict:
    keys = jax.random.split(jax.random.key(seed), 11)
    own_keys = jax.random.split(jax.random.fold_in(keys[10], part), 11)
    queries = draw_queries(jax.random.fold_in(jax.random.fold_in(keys[10], part), 71), part)
    new_keys = draw_new_keys(jax.random.fold_in(jax.random.fold_in(keys[10], part), 71), part)
    new_values = scatter_about(own_keys[2], (REQUESTS, STEPS, KVH, HD), 3.0, 12.0, ((0, 16),))
    suffix_keys = scatter_about(own_keys[3], (REQUESTS, SUF, KVH, HD), 2.0, 8.0, ((0, 16),))
    suffix_values = scatter_about(own_keys[4], (REQUESTS, SUF, KVH, HD), 3.0, 12.0, ((0, 16),))
    suffix_len = ragged_sizes(own_keys[5], REQUESTS, REQUESTS * SUF // 2, SUF, 2).astype(jnp.int32)
    prefix_keys = scatter_about(own_keys[6], (NBLK, BS, KVH, HD), 2.0, 8.0, ((0, 16),))
    prefix_values = scatter_about(own_keys[7], (NBLK, BS, KVH, HD), 3.0, 12.0, ((0, 16),))
    block_ids = jax.random.permutation(own_keys[8], NBLK).astype(jnp.int32)
    block_lists = different_ones(own_keys[9], REQUESTS, NBLK, NBR, 4096)
    return dict(queries=queries, new_keys=new_keys, new_values=new_values, suffix_keys=suffix_keys, suffix_values=suffix_values, suffix_len=suffix_len, prefix_keys=prefix_keys, prefix_values=prefix_values, block_ids=block_ids, block_lists=block_lists)


def reference(queries, new_keys, new_values, suffix_keys, suffix_values, suffix_len, prefix_keys, prefix_values, block_ids, block_lists):
    slot_of = jnp.zeros((NBLK,), jnp.int32).at[block_ids].set(jnp.arange(NBLK, dtype=jnp.int32))
    score_scale = 1.0 / math.sqrt(HD)
    prior_count = NBR * BS
    total_keys = prior_count + SUF + STEPS

    def one_request(packed):
        query_rows, fresh_keys, fresh_values, tail_keys, tail_values, tail_len, named = packed
        slots = slot_of[named].astype(jnp.int32)
        prior_keys = prefix_keys[slots].reshape(prior_count, KVH, HD)
        prior_values = prefix_values[slots].reshape(prior_count, KVH, HD)
        key_rows = jnp.concatenate([prior_keys, tail_keys, fresh_keys], axis=0).astype(jnp.float32)
        value_rows = jnp.concatenate([prior_values, tail_values, fresh_values], axis=0).astype(jnp.float32)
        position = jnp.arange(total_keys, dtype=jnp.int32)
        base_visible = (position < prior_count) | (position >= prior_count) & (position < prior_count + tail_len)
        fresh_index = position - prior_count - SUF
        step_index = jnp.arange(STEPS, dtype=jnp.int32)
        visible = base_visible[None, :] | (fresh_index[None, :] >= 0) & (fresh_index[None, :] <= step_index[:, None])
        expanded_keys = jnp.repeat(key_rows, GROUP, axis=1)
        expanded_values = jnp.repeat(value_rows, GROUP, axis=1)
        scores = jnp.einsum('shd,khd->shk', query_rows.astype(jnp.float32), expanded_keys) * score_scale
        shown = visible[:, None, :]
        row_top = lax.optimization_barrier(jnp.max(jnp.where(shown, scores, -jnp.inf), axis=-1, keepdims=True))
        weights = jnp.where(shown, jnp.exp(scores - row_top), 0.0)
        totals = lax.optimization_barrier(jnp.sum(weights, axis=-1))
        rounded = lax.optimization_barrier(weights.astype(jnp.bfloat16)).astype(jnp.float32)
        mixed = jnp.einsum('shk,khd->shd', rounded, expanded_values) / totals[..., None]
        return mixed.astype(jnp.bfloat16)
    return lax.map(one_request, (queries, new_keys, new_values, suffix_keys, suffix_values, suffix_len, block_lists))
```

```python
import functools
import math

import jax
import jax.numpy as jnp
from jax import lax
from jax.experimental import pallas as pl
from jax.experimental.pallas import tpu as pltpu
from jax.sharding import PartitionSpec as P

F32 = jnp.float32
BF16 = jnp.bfloat16
NT = (((1,), (1,)), ((), ()))


def fold_of(count):
    chips = count // 2
    inner = 1 << ((chips.bit_length() - 1) // 2)
    return chips // inner, inner


def attend_kernel(
    outer,
    inner,
    q_hbm,
    fk_ref,
    fv_ref,
    sk_hbm,
    sv_hbm,
    len_ref,
    pk_ref,
    pv_ref,
    id_ref,
    lists_ref,
    out_ref,
    q_ref,
    sk_ref,
    sv_ref,
    wide,
    kbuf,
    vbuf,
    ibuf,
    slot_v,
    slot_s,
    top,
    tot,
    acc,
    prob,
    load_sem,
    line_recv,
    core_recv,
    a_send,
    b_send,
    core_send,
):
    requests, steps, head_count, width = q_ref.shape

    key_heads = fk_ref.shape[0] // (requests * steps)
    block = pk_ref.shape[0] // key_heads
    group = head_count // key_heads
    rows = steps * group
    suffix = sk_ref.shape[1] // key_heads
    named = lists_ref.shape[0]
    factor = math.log2(math.e) / math.sqrt(width)
    bufs = (kbuf, ibuf, vbuf)

    me = lax.axis_index("loop")
    core = lax.rem(me, 2)
    chip = me // 2
    pa = chip // inner
    pb = lax.rem(chip, inner)

    def device(a, b, c):
        return {"loop": (a * inner + b) * 2 + c}

    loads = [pltpu.make_async_copy(q_hbm, q_ref, load_sem.at[0])]
    for r in range(requests):
        loads.append(pltpu.make_async_copy(sk_hbm.at[r], sk_ref.at[r], load_sem.at[1 + 2 * r]))
        loads.append(pltpu.make_async_copy(sv_hbm.at[r], sv_ref.at[r], load_sem.at[2 + 2 * r]))
    for copy in loads:
        copy.start()

    neighbours = [
        (pa > 0, (pa - 1, pb, core)),
        (pa < outer - 1, (pa + 1, pb, core)),
        (pb > 0, (pa, pb - 1, core)),
        (pb < inner - 1, (pa, pb + 1, core)),
    ]
    barrier = pltpu.get_barrier_semaphore()
    count = jnp.int32(1)
    pl.semaphore_signal(
        barrier, inc=1, device_id=device(pa, pb, 1 - core), device_id_type=pl.DeviceIdType.MESH
    )
    for there, where in neighbours:
        count = count + there.astype(jnp.int32)

        @pl.when(there)
        def _(where=where):
            pl.semaphore_signal(
                barrier, inc=1, device_id=device(*where), device_id_type=pl.DeviceIdType.MESH
            )

    def split_rows(value, area, per_head):
        size = per_head * key_heads
        wide[area, pl.ds(0, size), :] = value.astype(F32)
        return [
            wide[area, pl.ds(g, per_head, stride=key_heads), :].astype(BF16)
            for g in range(key_heads)
        ]

    mine = pa * inner + pb
    for area, (source, target) in enumerate(((pk_ref, kbuf), (pv_ref, vbuf))):
        parts = split_rows(source[...], area, block)
        for g in range(key_heads):
            target[core, mine, pl.ds(g * block, block), :] = parts[g]
    ibuf[core, mine] = jnp.full(ibuf.shape[2:], id_ref[0], jnp.int32)

    pl.semaphore_wait(barrier, count)

    pending = []

    def send(kind, a, b, sem, recv, condition, where):
        copy = pltpu.make_async_remote_copy(
            src_ref=bufs[kind].at[core, a * inner + b],
            dst_ref=bufs[kind].at[core, a * inner + b],
            send_sem=sem,
            recv_sem=recv,
            device_id=device(*where),
            device_id_type=pl.DeviceIdType.MESH,
        )

        @pl.when(condition)
        def _():
            copy.start()

        return condition, copy

    def send_a(kind, a, condition, up):
        where = (pa + 1, pb, core) if up else (pa - 1, pb, core)
        ok = condition & ((pa < outer - 1) if up else (pa > 0))
        slot = a * inner + pb
        pending.append(
            send(kind, a, pb, a_send.at[kind, int(up), a], line_recv.at[kind, slot], ok, where)
        )

    def send_b(kind, a, b, condition, up, keep=True):
        where = (pa, pb + 1, core) if up else (pa, pb - 1, core)
        ok = condition & ((pb < inner - 1) if up else (pb > 0))
        slot = a * inner + b
        entry = send(kind, a, b, b_send.at[kind, int(up), slot], line_recv.at[kind, slot], ok, where)
        if keep:
            pending.append(entry)
        return entry

    def send_core(kind, a, b, condition):
        send(
            kind, a, b, core_send.at[kind], core_recv.at[kind], condition, (pa, pb, 1 - core)
        )

    def arrived(kind, a, b, condition):
        slot = a * inner + b

        @pl.when(condition)
        def _():
            here = bufs[kind].at[core, slot]
            pltpu.make_async_copy(here, here, line_recv.at[kind, slot]).wait()

    always = pa >= 0

    def own(kinds):
        for kind in kinds:
            send_a(kind, pa, always, True)
            send_a(kind, pa, always, False)
            send_b(kind, pa, pb, always, True)
            send_b(kind, pa, pb, always, False)
        for kind in kinds:
            send_core(kind, pa, pb, always)

    def line_event(t, kinds):
        for up, condition, a in ((True, pa >= t, pa - t), (False, pa + t < outer, pa + t)):
            a = jnp.clip(a, 0, outer - 1)
            for kind in kinds:
                arrived(kind, a, pb, condition)
                send_a(kind, a, condition, up)
                send_b(kind, a, pb, condition, True)
                send_b(kind, a, pb, condition, False)
                send_core(kind, a, pb, condition)

    def cross_one(u, a, condition, kinds):
        for up, here, b in ((True, pb >= u, pb - u), (False, pb + u < inner, pb + u)):
            here = here & condition
            b = jnp.clip(b, 0, inner - 1)
            for kind in kinds:
                arrived(kind, a, b, here)
                send_b(kind, a, b, here, up, keep=False)
                send_core(kind, a, b, here)

    def cross_wait(u, a, condition, kinds):
        for up, here, b in ((True, pb >= u, pb - u), (False, pb + u < inner, pb + u)):
            ok = here & condition & ((pb < inner - 1) if up else (pb > 0))
            slot = a * inner + jnp.clip(b, 0, inner - 1)
            for kind in kinds:

                @pl.when(ok)
                def _(kind=kind, slot=slot, up=up):
                    piece = bufs[kind].at[core, slot]
                    pltpu.make_async_copy(piece, piece, b_send.at[kind, int(up), slot]).wait()

    def order(t):
        if t == 0:
            return [(always, pa)]
        return [
            (pa >= t, jnp.clip(pa - t, 0, outer - 1)),
            (pa + t < outer, jnp.clip(pa + t, 0, outer - 1)),
        ]

    def cross_event(u, t, kinds):
        for condition, a in order(t):
            cross_one(u, a, condition, kinds)

    def query_rows(r, g):
        return q_ref[r, :, pl.ds(g * group, group), :].reshape(rows, width)

    def fresh_unit():
        loads[0].wait()
        fresh = requests * steps
        keys = split_rows(fk_ref[...], 0, fresh)
        values = split_rows(fv_ref[...], 1, fresh)
        row = lax.broadcasted_iota(jnp.int32, (requests * rows, fresh), 0)
        col = lax.broadcasted_iota(jnp.int32, (requests * rows, fresh), 1)
        shown = (row // rows == col // steps) & (
            lax.rem(col, steps) <= lax.rem(row, rows) // group
        )
        for g in range(key_heads):
            q = q_ref[:, :, pl.ds(g * group, group), :].reshape(requests * rows, width)
            s = lax.dot_general(q, keys[g], NT, preferred_element_type=F32) * factor
            s = jnp.where(shown, s, -jnp.inf)
            m = jnp.max(s, axis=1, keepdims=True)
            p = jnp.exp2(s - m)
            l = jnp.sum(p, axis=1, keepdims=True)
            o = jnp.dot(p.astype(BF16), values[g], preferred_element_type=F32)
            shape = (requests, rows, width)
            top[:, g] = jnp.broadcast_to(m, (requests * rows, width)).reshape(shape)
            tot[:, g] = jnp.broadcast_to(l, (requests * rows, width)).reshape(shape)
            acc[:, g] = o.reshape(shape)

    def suffix_unit(r):
        loads[1 + 2 * r].wait()
        keys = split_rows(sk_ref[r], 0, suffix)
        loads[2 + 2 * r].wait()
        values = split_rows(sv_ref[r], 1, suffix)
        shown = lax.broadcasted_iota(jnp.int32, (rows, suffix), 1) < len_ref[r]
        for g in range(key_heads):
            s = lax.dot_general(query_rows(r, g), keys[g], NT, preferred_element_type=F32)
            s = jnp.where(shown, s * factor, -jnp.inf)
            before = top[r, g][:, :1]
            m = jnp.maximum(before, jnp.max(s, axis=1, keepdims=True))
            p = jnp.exp2(s - m)
            shrink = jnp.exp2(before - m)
            l = tot[r, g][:, :1] * shrink + jnp.sum(p, axis=1, keepdims=True)
            o = jnp.dot(p.astype(BF16), values[g], preferred_element_type=F32)
            top[r, g] = jnp.broadcast_to(m, (rows, width))
            tot[r, g] = jnp.broadcast_to(l, (rows, width))
            acc[r, g] = acc[r, g] * shrink + o

    K = (0, 1)
    V = (2,)
    events = [lambda: cross_event(1, 0, K)] if inner > 1 else []
    if inner > 1:
        events.append(lambda: cross_event(1, 0, V))
    for t in range(1, outer):
        events.append(lambda t=t: line_event(t, K))
        events.append(lambda t=t: line_event(t, V))
    if inner > 1:
        events = events[2:] + events[:2]
    units = [functools.partial(suffix_unit, r) for r in range(requests)]

    own(K)
    own(V)
    fresh_unit()
    units.pop(0)()
    while units or events:
        if units:
            units.pop(0)()
        if events:
            events.pop(0)()

    for t in range(1, outer):
        if inner > 1:
            cross_event(1, t, K)

    def far(u, kinds):
        for t in range(outer):
            cross_event(u, t, kinds)

    if inner > 2:
        pl.loop(2, inner)(lambda u: far(u, K))

    def whole_wait(kind, side, sem):
        half = bufs[kind].at[side]
        pltpu.make_async_copy(half, half, sem).wait()

    whole_wait(0, 1 - core, core_recv.at[0])
    whole_wait(1, 1 - core, core_recv.at[1])

    half = outer * inner
    ids = ibuf[:, :, 0, :].reshape(2 * half, width)[:, :requests]
    place = lax.broadcasted_iota(jnp.int32, ids.shape, 0)
    for j in range(named):
        match = ids == lists_ref[pl.ds(j, 1), :]
        slot_v[pl.ds(j, 1), pl.ds(0, requests)] = jnp.max(
            jnp.where(match, place, 0), axis=0, keepdims=True
        )
    to_scalar = pltpu.make_async_copy(slot_v, slot_s, load_sem.at[0])
    to_scalar.start()
    to_scalar.wait()

    def gathered(buf, r, g):
        parts = []
        for j in range(named):
            slot = slot_s[j, r]
            parts.append(buf[slot // half, lax.rem(slot, half), pl.ds(g * block, block), :])
        return jnp.concatenate(parts, axis=0)

    @pl.loop(0, requests)
    def _(r):
        for g in range(key_heads):
            s = lax.dot_general(
                query_rows(r, g), gathered(kbuf, r, g), NT, preferred_element_type=F32
            )
            s = s * factor
            before = top[r, g][:, :1]
            m = jnp.maximum(before, jnp.max(s, axis=1, keepdims=True))
            p = jnp.exp2(s - m)
            shrink = jnp.exp2(before - m)
            l = tot[r, g][:, :1] * shrink + jnp.sum(p, axis=1, keepdims=True)
            prob[r, g] = p.astype(BF16)
            tot[r, g] = jnp.broadcast_to(l, (rows, width))
            acc[r, g] = acc[r, g] * shrink

    for t in range(1, outer):
        if inner > 1:
            cross_event(1, t, V)
    if inner > 2:
        pl.loop(2, inner)(lambda u: far(u, V))
    whole_wait(2, 1 - core, core_recv.at[2])

    @pl.loop(0, requests)
    def _(r):
        for g in range(key_heads):
            o = acc[r, g] + jnp.dot(
                prob[r, g], gathered(vbuf, r, g), preferred_element_type=F32
            )
            o = (o / tot[r, g]).astype(BF16)
            out_ref[r, :, pl.ds(g * group, group), :] = o.reshape(steps, group, width)

    for condition, copy in pending:

        @pl.when(condition)
        def _(copy=copy):
            copy.wait_send()

    if inner > 1:
        def drain(u):
            for t in range(outer):
                for condition, a in order(t):
                    cross_wait(u, a, condition, (0, 1, 2))

        if inner > 2:
            pl.loop(1, inner)(drain)
    for kind in range(3):
        whole_wait(kind, core, core_send.at[kind])


def per_device(
    loop,
    queries,
    new_keys,
    new_values,
    suffix_keys,
    suffix_values,
    suffix_len,
    prefix_keys,
    prefix_values,
    block_ids,
    block_lists,
):
    outer, inner = fold_of(loop)
    requests, steps, head_count, width = queries.shape
    key_heads = new_keys.shape[2]
    suffix = suffix_keys.shape[1]
    block = prefix_keys.shape[1]
    named = block_lists.shape[1]
    rows = steps * head_count // key_heads
    half = outer * inner
    vmem = pl.BlockSpec(memory_space=pltpu.VMEM)
    smem = pl.BlockSpec(memory_space=pltpu.SMEM)
    anywhere = pl.BlockSpec(memory_space=pltpu.HBM)
    kernel = functools.partial(attend_kernel, outer, inner)
    return pl.pallas_call(
        kernel,
        out_shape=jax.ShapeDtypeStruct(queries.shape, queries.dtype),
        in_specs=[
            anywhere,
            vmem,
            vmem,
            anywhere,
            anywhere,
            smem,
            vmem,
            vmem,
            smem,
            vmem,
        ],
        out_specs=vmem,
        scratch_shapes=[
            pltpu.VMEM(queries.shape, BF16),
            pltpu.VMEM((requests, suffix * key_heads, width), BF16),
            pltpu.VMEM((requests, suffix * key_heads, width), BF16),
            pltpu.VMEM((2, max(suffix, block, requests * steps) * key_heads, width), F32),
            pltpu.VMEM((2, half, key_heads * block, width), BF16),
            pltpu.VMEM((2, half, key_heads * block, width), BF16),
            pltpu.VMEM((2, half, 8, width), jnp.int32),
            pltpu.VMEM((8, 128), jnp.int32),
            pltpu.SMEM((8, 128), jnp.int32),
            pltpu.VMEM((requests, key_heads, rows, width), F32),
            pltpu.VMEM((requests, key_heads, rows, width), F32),
            pltpu.VMEM((requests, key_heads, rows, width), F32),
            pltpu.VMEM((requests, key_heads, rows, named * block), BF16),
            pltpu.SemaphoreType.DMA((1 + 2 * requests,)),
            pltpu.SemaphoreType.DMA((3, half)),
            pltpu.SemaphoreType.DMA((3,)),
            pltpu.SemaphoreType.DMA((3, 2, outer)),
            pltpu.SemaphoreType.DMA((3, 2, half)),
            pltpu.SemaphoreType.DMA((3,)),
        ],
        compiler_params=pltpu.CompilerParams(
            collective_id=0, has_side_effects=True, vmem_limit_bytes=60 * 1024 * 1024
        ),
        name="attend",
    )(
        queries,
        new_keys.reshape(-1, width),
        new_values.reshape(-1, width),
        suffix_keys.reshape(requests, suffix * key_heads, width),
        suffix_values.reshape(requests, suffix * key_heads, width),
        suffix_len,
        prefix_keys.reshape(-1, width),
        prefix_values.reshape(-1, width),
        block_ids,
        block_lists.T,
    )


def solution(mesh):
    lead = ("groups", "loop")
    in_specs = (
        P(lead, None, None, None),
        P(lead, None, None, None),
        P(lead, None, None, None),
        P(lead, None, None, None),
        P(lead, None, None, None),
        P(lead),
        P(lead, None, None, None),
        P(lead, None, None, None),
        P(lead),
        P(lead, None),
    )
    return jax.shard_map(
        functools.partial(per_device, mesh.shape["loop"]),
        mesh=mesh,
        in_specs=in_specs,
        out_specs=P(lead, None, None, None),
        check_vma=False,
    )
```

```python
import functools
import math

import jax
import jax.numpy as jnp
from jax import lax
from jax.experimental import pallas as pl
from jax.experimental.pallas import tpu as pltpu
from jax.sharding import PartitionSpec as P

F32 = jnp.float32
BF16 = jnp.bfloat16
NT = (((1,), (1,)), ((), ()))


def fold_of(count):
    chips = count // 2
    inner = 1 << ((chips.bit_length() - 1) // 2)
    return chips // inner, inner


def attend_kernel(
    outer,
    inner,
    q_hbm,
    fk_hbm,
    fv_hbm,
    sk_hbm,
    sv_hbm,
    len_hbm,
    pk_hbm,
    pv_hbm,
    id_ref,
    lists_hbm,
    out_ref,
    fk_ref,
    fv_ref,
    pk_ref,
    pv_ref,
    lists_ref,
    len_ref,
    fresh_k,
    fresh_v,
    q_ref,
    sk_ref,
    sv_ref,
    wide,
    kbuf,
    vbuf,
    ibuf,
    slot_v,
    slot_s,
    top,
    tot,
    acc,
    prob,
    load_sem,
    small_sem,
    line_recv,
    core_recv,
    a_send,
    b_send,
    core_send,
):
    requests, steps, head_count, width = q_ref.shape

    key_heads = fk_ref.shape[0] // (requests * steps)
    block = pk_ref.shape[0] // key_heads
    group = head_count // key_heads
    rows = steps * group
    suffix = sk_ref.shape[1] // key_heads
    named = lists_ref.shape[0]
    factor = math.log2(math.e) / math.sqrt(width)
    bufs = (kbuf, ibuf, vbuf)

    me = lax.axis_index("loop")
    core = lax.rem(me, 2)
    chip = me // 2
    pa = chip // inner
    pb = lax.rem(chip, inner)

    def device(a, b, c):
        return {"loop": (a * inner + b) * 2 + c}

    pairs = (
        (fk_hbm, fk_ref),
        (fv_hbm, fv_ref),
        (pk_hbm, pk_ref),
        (pv_hbm, pv_ref),
        (lists_hbm, lists_ref),
        (len_hbm, len_ref),
    )
    small = [pltpu.make_async_copy(a, b, small_sem.at[i]) for i, (a, b) in enumerate(pairs)]
    for i in (2, 3, 0, 1, 5, 4):
        small[i].start()
    loads = [pltpu.make_async_copy(q_hbm, q_ref, load_sem.at[0])]
    for r in range(requests):
        loads.append(pltpu.make_async_copy(sk_hbm.at[r], sk_ref.at[r], load_sem.at[1 + 2 * r]))
        loads.append(pltpu.make_async_copy(sv_hbm.at[r], sv_ref.at[r], load_sem.at[2 + 2 * r]))
    for copy in loads:
        copy.start()

    neighbours = [
        (pa > 0, (pa - 1, pb, core)),
        (pa < outer - 1, (pa + 1, pb, core)),
        (pb > 0, (pa, pb - 1, core)),
        (pb < inner - 1, (pa, pb + 1, core)),
    ]
    barrier = pltpu.get_barrier_semaphore()
    count = jnp.int32(1)
    pl.semaphore_signal(
        barrier, inc=1, device_id=device(pa, pb, 1 - core), device_id_type=pl.DeviceIdType.MESH
    )
    for there, where in neighbours:
        count = count + there.astype(jnp.int32)

        @pl.when(there)
        def _(where=where):
            pl.semaphore_signal(
                barrier, inc=1, device_id=device(*where), device_id_type=pl.DeviceIdType.MESH
            )

    def split_rows(value, area, per_head):
        size = per_head * key_heads
        wide[area, pl.ds(0, size), :] = value.astype(F32)
        return [
            wide[area, pl.ds(g, per_head, stride=key_heads), :].astype(BF16)
            for g in range(key_heads)
        ]

    mine = pa * inner + pb
    for area, (source, target) in enumerate(((pk_ref, kbuf), (pv_ref, vbuf))):
        small[2 + area].wait()
        parts = split_rows(source[...], area, block)
        for g in range(key_heads):
            target[core, mine, pl.ds(g * block, block), :] = parts[g]
    ibuf[core, mine] = jnp.full(ibuf.shape[2:], id_ref[0], jnp.int32)

    pl.semaphore_wait(barrier, count)

    pending = []

    def send(kind, a, b, sem, recv, condition, where):
        copy = pltpu.make_async_remote_copy(
            src_ref=bufs[kind].at[core, a * inner + b],
            dst_ref=bufs[kind].at[core, a * inner + b],
            send_sem=sem,
            recv_sem=recv,
            device_id=device(*where),
            device_id_type=pl.DeviceIdType.MESH,
        )

        @pl.when(condition)
        def _():
            copy.start()

        return condition, copy

    def send_a(kind, a, condition, up):
        where = (pa + 1, pb, core) if up else (pa - 1, pb, core)
        ok = condition & ((pa < outer - 1) if up else (pa > 0))
        slot = a * inner + pb
        pending.append(
            send(kind, a, pb, a_send.at[kind, int(up), a], line_recv.at[kind, slot], ok, where)
        )

    def send_b(kind, a, b, condition, up, keep=True):
        where = (pa, pb + 1, core) if up else (pa, pb - 1, core)
        ok = condition & ((pb < inner - 1) if up else (pb > 0))
        slot = a * inner + b
        entry = send(kind, a, b, b_send.at[kind, int(up), slot], line_recv.at[kind, slot], ok, where)
        if keep:
            pending.append(entry)
        return entry

    def send_core(kind, a, b, condition):
        send(
            kind, a, b, core_send.at[kind], core_recv.at[kind], condition, (pa, pb, 1 - core)
        )

    def arrived(kind, a, b, condition):
        slot = a * inner + b

        @pl.when(condition)
        def _():
            here = bufs[kind].at[core, slot]
            pltpu.make_async_copy(here, here, line_recv.at[kind, slot]).wait()

    always = pa >= 0

    def own(kinds):
        for kind in kinds:
            send_a(kind, pa, always, True)
            send_a(kind, pa, always, False)
            send_b(kind, pa, pb, always, True)
            send_b(kind, pa, pb, always, False)
        for kind in kinds:
            send_core(kind, pa, pb, always)

    def line_event(t, kinds):
        for up, condition, a in ((True, pa >= t, pa - t), (False, pa + t < outer, pa + t)):
            a = jnp.clip(a, 0, outer - 1)
            for kind in kinds:
                arrived(kind, a, pb, condition)
                send_a(kind, a, condition, up)
                send_b(kind, a, pb, condition, True)
                send_b(kind, a, pb, condition, False)
                send_core(kind, a, pb, condition)

    def cross_one(u, a, condition, kinds):
        for up, here, b in ((True, pb >= u, pb - u), (False, pb + u < inner, pb + u)):
            here = here & condition
            b = jnp.clip(b, 0, inner - 1)
            for kind in kinds:
                arrived(kind, a, b, here)
                send_b(kind, a, b, here, up, keep=False)
                send_core(kind, a, b, here)

    def cross_wait(u, a, condition, kinds):
        for up, here, b in ((True, pb >= u, pb - u), (False, pb + u < inner, pb + u)):
            ok = here & condition & ((pb < inner - 1) if up else (pb > 0))
            slot = a * inner + jnp.clip(b, 0, inner - 1)
            for kind in kinds:

                @pl.when(ok)
                def _(kind=kind, slot=slot, up=up):
                    piece = bufs[kind].at[core, slot]
                    pltpu.make_async_copy(piece, piece, b_send.at[kind, int(up), slot]).wait()

    def order(t):
        if t == 0:
            return [(always, pa)]
        return [
            (pa >= t, jnp.clip(pa - t, 0, outer - 1)),
            (pa + t < outer, jnp.clip(pa + t, 0, outer - 1)),
        ]

    def cross_event(u, t, kinds):
        for condition, a in order(t):
            cross_one(u, a, condition, kinds)

    def query_rows(r, g):
        return q_ref[r, :, pl.ds(g * group, group), :].reshape(rows, width)

    def wide_max(parts):
        best = functools.reduce(jnp.maximum, parts)
        return jnp.broadcast_to(jnp.max(best, axis=1, keepdims=True), best.shape)

    def columns(x):
        return [x[:, i : i + width] for i in range(0, x.shape[1], width)]

    def fresh_unit():
        fresh = requests * steps
        small[0].wait()
        small[1].wait()
        keys = split_rows(fk_ref[...], 0, fresh)
        values = split_rows(fv_ref[...], 1, fresh)
        for part, held in ((keys, fresh_k), (values, fresh_v)):
            held[...] = jnp.zeros_like(held)
            for g in range(key_heads):
                held[g, pl.ds(0, fresh), :] = part[g]
        loads[0].wait()
        small[5].wait()

    def suffix_unit(r):
        loads[1 + 2 * r].wait()
        keys = split_rows(sk_ref[r], 0, suffix)
        loads[2 + 2 * r].wait()
        values = split_rows(sv_ref[r], 1, suffix)
        slot = lax.broadcasted_iota(jnp.int32, (8, suffix), 1)
        hidden = jnp.where(slot < len_ref[r], 0.0, -jnp.inf)
        hidden = jnp.concatenate([hidden] * (rows // 8), axis=0)
        row = lax.broadcasted_iota(jnp.int32, (rows, fresh_k.shape[1]), 0)
        col = lax.broadcasted_iota(jnp.int32, (rows, fresh_k.shape[1]), 1) - r * steps
        own_hidden = jnp.where((col >= 0) & (col <= row // group), 0.0, -jnp.inf)
        biases = columns(hidden) + columns(own_hidden)
        for g in range(key_heads):
            all_keys = jnp.concatenate([keys[g], fresh_k[g]], axis=0)
            all_values = jnp.concatenate([values[g], fresh_v[g]], axis=0)
            s = lax.dot_general(query_rows(r, g), all_keys, NT, preferred_element_type=F32)
            s = [x * factor + bias for x, bias in zip(columns(s), biases)]
            m = wide_max(s)
            p = [jnp.exp2(x - m) for x in s]
            top[r, g] = m
            tot[r, g] = functools.reduce(jnp.add, p)
            p = jnp.concatenate(p, axis=1).astype(BF16)
            acc[r, g] = jnp.dot(p, all_values, preferred_element_type=F32)

    K = (0, 1)
    V = (2,)
    events = []
    for t in range(1, outer):
        events.append(lambda t=t: line_event(t, K))
        events.append(lambda t=t: line_event(t, V))
    if inner > 1:
        events.append(lambda: (cross_event(1, 0, K), cross_event(1, 0, V)))
    units = [functools.partial(suffix_unit, r) for r in range(requests)]

    own(K)
    own(V)
    fresh_unit()
    while units or events:
        if units:
            units.pop(0)()
        if events:
            events.pop(0)()

    for t in range(1, outer):
        if inner > 1:
            cross_event(1, t, K)

    def far(u, kinds):
        for t in range(outer):
            cross_event(u, t, kinds)

    if inner > 2:
        pl.loop(2, inner)(lambda u: far(u, K))

    def whole_wait(kind, side, sem):
        half = bufs[kind].at[side]
        pltpu.make_async_copy(half, half, sem).wait()

    whole_wait(0, 1 - core, core_recv.at[0])
    whole_wait(1, 1 - core, core_recv.at[1])

    half = outer * inner
    ids = ibuf[:, :, 0, :].reshape(2 * half, width)[:, :requests]
    place = lax.broadcasted_iota(jnp.int32, ids.shape, 0)
    small[4].wait()
    for j in range(named):
        match = ids == lists_ref[pl.ds(j, 1), :]
        slot_v[pl.ds(j, 1), pl.ds(0, requests)] = jnp.max(
            jnp.where(match, place, 0), axis=0, keepdims=True
        )
    to_scalar = pltpu.make_async_copy(slot_v, slot_s, load_sem.at[0])
    to_scalar.start()
    to_scalar.wait()

    def gathered(buf, r, g):
        parts = []
        for j in range(named):
            slot = slot_s[j, r]
            parts.append(buf[slot // half, lax.rem(slot, half), pl.ds(g * block, block), :])
        return jnp.concatenate(parts, axis=0)

    def prior_unit(r):
        for g in range(key_heads):
            s = lax.dot_general(
                query_rows(r, g), gathered(kbuf, r, g), NT, preferred_element_type=F32
            )
            s = [x * factor for x in columns(s)]
            before = top[r, g]
            m = jnp.maximum(before, wide_max(s))
            p = [jnp.exp2(x - m) for x in s]
            shrink = jnp.exp2(before - m)
            l = functools.reduce(jnp.add, p, tot[r, g] * shrink)
            l = 1.0 / jnp.broadcast_to(jnp.sum(l, axis=1, keepdims=True), l.shape)
            prob[r, g] = jnp.concatenate(p, axis=1).astype(BF16)
            tot[r, g] = l
            acc[r, g] = acc[r, g] * (shrink * l)

    late = [lambda t=t: cross_event(1, t, V) for t in range(1, outer)] if inner > 1 else []
    for r in range(requests):
        prior_unit(r)
        if late and r % 2 == 1:
            late.pop(0)()
    while late:
        late.pop(0)()
    if inner > 2:
        pl.loop(2, inner)(lambda u: far(u, V))
    whole_wait(2, 1 - core, core_recv.at[2])

    for r in range(requests):
        for g in range(key_heads):
            o = jnp.dot(prob[r, g], gathered(vbuf, r, g), preferred_element_type=F32)
            o = (acc[r, g] + o * tot[r, g]).astype(BF16)
            out_ref[r, :, pl.ds(g * group, group), :] = o.reshape(steps, group, width)

    for condition, copy in pending:

        @pl.when(condition)
        def _(copy=copy):
            copy.wait_send()

    if inner > 1:
        def drain(u):
            for t in range(outer):
                for condition, a in order(t):
                    cross_wait(u, a, condition, (0, 1, 2))

        if inner > 2:
            pl.loop(1, inner)(drain)
    for kind in range(3):
        whole_wait(kind, core, core_send.at[kind])


def per_device(
    loop,
    queries,
    new_keys,
    new_values,
    suffix_keys,
    suffix_values,
    suffix_len,
    prefix_keys,
    prefix_values,
    block_ids,
    block_lists,
):
    outer, inner = fold_of(loop)
    requests, steps, head_count, width = queries.shape
    key_heads = new_keys.shape[2]
    suffix = suffix_keys.shape[1]
    block = prefix_keys.shape[1]
    named = block_lists.shape[1]
    rows = steps * head_count // key_heads
    half = outer * inner
    padded = -(-requests * steps // width) * width
    vmem = pl.BlockSpec(memory_space=pltpu.VMEM)
    smem = pl.BlockSpec(memory_space=pltpu.SMEM)
    anywhere = pl.BlockSpec(memory_space=pltpu.HBM)
    kernel = functools.partial(attend_kernel, outer, inner)
    return pl.pallas_call(
        kernel,
        out_shape=jax.ShapeDtypeStruct(queries.shape, queries.dtype),
        in_specs=[anywhere] * 8 + [smem, anywhere],
        out_specs=vmem,
        scratch_shapes=[
            pltpu.VMEM((requests * steps * key_heads, width), BF16),
            pltpu.VMEM((requests * steps * key_heads, width), BF16),
            pltpu.VMEM((block * key_heads, width), BF16),
            pltpu.VMEM((block * key_heads, width), BF16),
            pltpu.VMEM((named, requests), jnp.int32),
            pltpu.SMEM((requests,), jnp.int32),
            pltpu.VMEM((key_heads, padded, width), BF16),
            pltpu.VMEM((key_heads, padded, width), BF16),
            pltpu.VMEM(queries.shape, BF16),
            pltpu.VMEM((requests, suffix * key_heads, width), BF16),
            pltpu.VMEM((requests, suffix * key_heads, width), BF16),
            pltpu.VMEM((2, max(suffix, block, requests * steps) * key_heads, width), F32),
            pltpu.VMEM((2, half, key_heads * block, width), BF16),
            pltpu.VMEM((2, half, key_heads * block, width), BF16),
            pltpu.VMEM((2, half, 8, width), jnp.int32),
            pltpu.VMEM((8, 128), jnp.int32),
            pltpu.SMEM((8, 128), jnp.int32),
            pltpu.VMEM((requests, key_heads, rows, width), F32),
            pltpu.VMEM((requests, key_heads, rows, width), F32),
            pltpu.VMEM((requests, key_heads, rows, width), F32),
            pltpu.VMEM((requests, key_heads, rows, named * block), BF16),
            pltpu.SemaphoreType.DMA((1 + 2 * requests,)),
            pltpu.SemaphoreType.DMA((6,)),
            pltpu.SemaphoreType.DMA((3, half)),
            pltpu.SemaphoreType.DMA((3,)),
            pltpu.SemaphoreType.DMA((3, 2, outer)),
            pltpu.SemaphoreType.DMA((3, 2, half)),
            pltpu.SemaphoreType.DMA((3,)),
        ],
        compiler_params=pltpu.CompilerParams(
            collective_id=0, has_side_effects=True, vmem_limit_bytes=60 * 1024 * 1024
        ),
        name="attend",
    )(
        queries,
        new_keys.reshape(-1, width),
        new_values.reshape(-1, width),
        suffix_keys.reshape(requests, suffix * key_heads, width),
        suffix_values.reshape(requests, suffix * key_heads, width),
        suffix_len,
        prefix_keys.reshape(-1, width),
        prefix_values.reshape(-1, width),
        block_ids,
        block_lists.T,
    )


def solution(mesh):
    lead = ("groups", "loop")
    in_specs = (
        P(lead, None, None, None),
        P(lead, None, None, None),
        P(lead, None, None, None),
        P(lead, None, None, None),
        P(lead, None, None, None),
        P(lead),
        P(lead, None, None, None),
        P(lead, None, None, None),
        P(lead),
        P(lead, None),
    )
    return jax.shard_map(
        functools.partial(per_device, mesh.shape["loop"]),
        mesh=mesh,
        in_specs=in_specs,
        out_specs=P(lead, None, None, None),
        check_vma=False,
    )
```

```python
import functools
import math

import jax
import jax.numpy as jnp
from jax import lax
from jax.experimental import pallas as pl
from jax.experimental.pallas import tpu as pltpu
from jax.sharding import PartitionSpec as P

F32 = jnp.float32
BF16 = jnp.bfloat16
NT = (((1,), (1,)), ((), ()))


def fold_of(count):
    chips = count // 2
    inner = 1 << ((chips.bit_length() - 1) // 2)
    return chips // inner, inner


def attend_kernel(
    outer,
    inner,
    q_hbm,
    fk_hbm,
    fv_hbm,
    sk_hbm,
    sv_hbm,
    len_hbm,
    pk_hbm,
    pv_hbm,
    id_ref,
    lists_hbm,
    out_ref,
    fk_ref,
    fv_ref,
    pk_ref,
    pv_ref,
    lists_ref,
    len_ref,
    fresh_k,
    fresh_v,
    q_ref,
    sk_ref,
    sv_ref,
    wide,
    kbuf,
    vbuf,
    ibuf,
    slot_v,
    slot_s,
    top,
    tot,
    acc,
    prob,
    load_sem,
    small_sem,
    line_recv,
    core_recv,
    a_send,
    b_send,
    core_send,
):
    requests, steps, head_count, width = q_ref.shape

    key_heads = fk_ref.shape[0] // (requests * steps)
    block = pk_ref.shape[0] // key_heads
    group = head_count // key_heads
    rows = steps * group
    suffix = sk_ref.shape[1] // key_heads
    named = lists_ref.shape[0]
    factor = math.log2(math.e) / math.sqrt(width)
    bufs = (kbuf, ibuf, vbuf)

    me = lax.axis_index("loop")
    core = lax.rem(me, 2)
    chip = me // 2
    pa = chip // inner
    pb = lax.rem(chip, inner)

    def device(a, b, c):
        return {"loop": (a * inner + b) * 2 + c}

    pairs = (
        (fk_hbm, fk_ref),
        (fv_hbm, fv_ref),
        (pk_hbm, pk_ref),
        (pv_hbm, pv_ref),
        (lists_hbm, lists_ref),
        (len_hbm, len_ref),
    )
    small = [pltpu.make_async_copy(a, b, small_sem.at[i]) for i, (a, b) in enumerate(pairs)]
    for i in (2, 3, 0, 1, 5, 4):
        small[i].start()
    loads = [pltpu.make_async_copy(q_hbm, q_ref, load_sem.at[0])]
    for r in range(requests):
        loads.append(pltpu.make_async_copy(sk_hbm.at[r], sk_ref.at[r], load_sem.at[1 + 2 * r]))
        loads.append(pltpu.make_async_copy(sv_hbm.at[r], sv_ref.at[r], load_sem.at[2 + 2 * r]))
    for copy in loads:
        copy.start()

    neighbours = [
        (pa > 0, (pa - 1, pb, core)),
        (pa < outer - 1, (pa + 1, pb, core)),
        (pb > 0, (pa, pb - 1, core)),
        (pb < inner - 1, (pa, pb + 1, core)),
    ]
    barrier = pltpu.get_barrier_semaphore()
    count = jnp.int32(1)
    pl.semaphore_signal(
        barrier, inc=1, device_id=device(pa, pb, 1 - core), device_id_type=pl.DeviceIdType.MESH
    )
    for there, where in neighbours:
        count = count + there.astype(jnp.int32)

        @pl.when(there)
        def _(where=where):
            pl.semaphore_signal(
                barrier, inc=1, device_id=device(*where), device_id_type=pl.DeviceIdType.MESH
            )

    def split_rows(value, area, per_head):
        size = per_head * key_heads
        wide[area, pl.ds(0, size), :] = value.astype(F32)
        return [
            wide[area, pl.ds(g, per_head, stride=key_heads), :].astype(BF16)
            for g in range(key_heads)
        ]

    mine = pa * inner + pb
    for area, (source, target) in enumerate(((pk_ref, kbuf), (pv_ref, vbuf))):
        small[2 + area].wait()
        parts = split_rows(source[...], area, block)
        for g in range(key_heads):
            target[core, mine, pl.ds(g * block, block), :] = parts[g]
    ibuf[core, mine] = jnp.full(ibuf.shape[2:], id_ref[0], jnp.int32)


    pending = []

    def send(kind, a, b, sem, recv, condition, where):
        copy = pltpu.make_async_remote_copy(
            src_ref=bufs[kind].at[core, a * inner + b],
            dst_ref=bufs[kind].at[core, a * inner + b],
            send_sem=sem,
            recv_sem=recv,
            device_id=device(*where),
            device_id_type=pl.DeviceIdType.MESH,
        )

        @pl.when(condition)
        def _():
            copy.start()

        return condition, copy

    def send_a(kind, a, condition, up):
        where = (pa + 1, pb, core) if up else (pa - 1, pb, core)
        ok = condition & ((pa < outer - 1) if up else (pa > 0))
        slot = a * inner + pb
        pending.append(
            send(kind, a, pb, a_send.at[kind, int(up), a], line_recv.at[kind, slot], ok, where)
        )

    def send_b(kind, a, b, condition, up, keep=True):
        where = (pa, pb + 1, core) if up else (pa, pb - 1, core)
        ok = condition & ((pb < inner - 1) if up else (pb > 0))
        slot = a * inner + b
        entry = send(kind, a, b, b_send.at[kind, int(up), slot], line_recv.at[kind, slot], ok, where)
        if keep:
            pending.append(entry)
        return entry

    def send_core(kind, a, b, condition):
        send(
            kind, a, b, core_send.at[kind], core_recv.at[kind], condition, (pa, pb, 1 - core)
        )

    def arrived(kind, a, b, condition):
        slot = a * inner + b

        @pl.when(condition)
        def _():
            here = bufs[kind].at[core, slot]
            pltpu.make_async_copy(here, here, line_recv.at[kind, slot]).wait()

    always = pa >= 0

    def own(kinds):
        for kind in kinds:
            send_a(kind, pa, always, True)
            send_a(kind, pa, always, False)
            send_b(kind, pa, pb, always, True)
            send_b(kind, pa, pb, always, False)
        for kind in kinds:
            send_core(kind, pa, pb, always)

    def line_event(t, kinds):
        for up, condition, a in ((True, pa >= t, pa - t), (False, pa + t < outer, pa + t)):
            a = jnp.clip(a, 0, outer - 1)
            for kind in kinds:
                arrived(kind, a, pb, condition)
                send_a(kind, a, condition, up)
                send_b(kind, a, pb, condition, True)
                send_b(kind, a, pb, condition, False)
                send_core(kind, a, pb, condition)

    def cross_one(u, a, condition, kinds):
        for up, here, b in ((True, pb >= u, pb - u), (False, pb + u < inner, pb + u)):
            here = here & condition
            b = jnp.clip(b, 0, inner - 1)
            for kind in kinds:
                arrived(kind, a, b, here)
                send_b(kind, a, b, here, up, keep=False)
                send_core(kind, a, b, here)

    def cross_wait(u, a, condition, kinds):
        for up, here, b in ((True, pb >= u, pb - u), (False, pb + u < inner, pb + u)):
            ok = here & condition & ((pb < inner - 1) if up else (pb > 0))
            slot = a * inner + jnp.clip(b, 0, inner - 1)
            for kind in kinds:

                @pl.when(ok)
                def _(kind=kind, slot=slot, up=up):
                    piece = bufs[kind].at[core, slot]
                    pltpu.make_async_copy(piece, piece, b_send.at[kind, int(up), slot]).wait()

    def order(t):
        if t == 0:
            return [(always, pa)]
        return [
            (pa >= t, jnp.clip(pa - t, 0, outer - 1)),
            (pa + t < outer, jnp.clip(pa + t, 0, outer - 1)),
        ]

    def cross_event(u, t, kinds):
        for condition, a in order(t):
            cross_one(u, a, condition, kinds)

    def query_rows(r, g):
        return q_ref[r, :, pl.ds(g * group, group), :].reshape(rows, width)

    def wide_max(parts):
        best = functools.reduce(jnp.maximum, parts)
        return jnp.broadcast_to(jnp.max(best, axis=1, keepdims=True), best.shape)

    def columns(x):
        return [x[:, i : i + width] for i in range(0, x.shape[1], width)]

    def fresh_unit():
        fresh = requests * steps
        small[0].wait()
        small[1].wait()
        keys = split_rows(fk_ref[...], 0, fresh)
        values = split_rows(fv_ref[...], 1, fresh)
        for part, held in ((keys, fresh_k), (values, fresh_v)):
            held[...] = jnp.zeros_like(held)
            for g in range(key_heads):
                held[g, pl.ds(0, fresh), :] = part[g]
        loads[0].wait()
        small[5].wait()

    def suffix_unit(r):
        loads[1 + 2 * r].wait()
        keys = split_rows(sk_ref[r], 0, suffix)
        loads[2 + 2 * r].wait()
        values = split_rows(sv_ref[r], 1, suffix)
        slot = lax.broadcasted_iota(jnp.int32, (8, suffix), 1)
        hidden = jnp.where(slot < len_ref[r], 0.0, -jnp.inf)
        hidden = jnp.concatenate([hidden] * (rows // 8), axis=0)
        row = lax.broadcasted_iota(jnp.int32, (rows, fresh_k.shape[1]), 0)
        col = lax.broadcasted_iota(jnp.int32, (rows, fresh_k.shape[1]), 1) - r * steps
        own_hidden = jnp.where((col >= 0) & (col <= row // group), 0.0, -jnp.inf)
        biases = columns(hidden) + columns(own_hidden)
        for g in range(key_heads):
            all_keys = jnp.concatenate([keys[g], fresh_k[g]], axis=0)
            all_values = jnp.concatenate([values[g], fresh_v[g]], axis=0)
            s = lax.dot_general(query_rows(r, g), all_keys, NT, preferred_element_type=F32)
            s = [x * factor + bias for x, bias in zip(columns(s), biases)]
            m = wide_max(s)
            p = [jnp.exp2(x - m) for x in s]
            top[r, g] = m
            tot[r, g] = functools.reduce(jnp.add, p)
            p = jnp.concatenate(p, axis=1).astype(BF16)
            acc[r, g] = jnp.dot(p, all_values, preferred_element_type=F32)

    K = (0, 1)
    V = (2,)
    crossing = inner > 1
    lines, cross_keys = [], []
    for t in range(1, outer):
        lines.append(lambda t=t: line_event(t, K))
        if t > 1:
            lines.append(lambda t=t: line_event(t - 1, V))
    early = []
    if crossing:
        early.append((3, lambda: cross_event(1, 0, K)))
        early.append((7, lambda: cross_event(1, 1, K)))
    for i, event in enumerate(lines):
        early.append((2 + i + (i > 0), event))
    early.sort(key=lambda entry: entry[0])

    fresh_unit()
    pl.semaphore_wait(barrier, count)
    own(K)
    own(V)
    for r in range(requests):
        suffix_unit(r)
        while early and early[0][0] <= r:
            early.pop(0)[1]()
    for _, event in early:
        event()
    if crossing:
        for t in range(2, outer):
            cross_event(1, t, K)

    def far(u, kinds):
        for t in range(outer):
            cross_event(u, t, kinds)

    if inner > 2:
        pl.loop(2, inner)(lambda u: far(u, K))

    def whole_wait(kind, side, sem):
        half = bufs[kind].at[side]
        pltpu.make_async_copy(half, half, sem).wait()

    whole_wait(0, 1 - core, core_recv.at[0])
    whole_wait(1, 1 - core, core_recv.at[1])

    half = outer * inner
    ids = ibuf[:, :, 0, :].reshape(2 * half, width)[:, :requests]
    place = lax.broadcasted_iota(jnp.int32, ids.shape, 0)
    small[4].wait()
    for j in range(named):
        match = ids == lists_ref[pl.ds(j, 1), :]
        slot_v[pl.ds(j, 1), pl.ds(0, requests)] = jnp.max(
            jnp.where(match, place, 0), axis=0, keepdims=True
        )
    to_scalar = pltpu.make_async_copy(slot_v, slot_s, load_sem.at[0])
    to_scalar.start()
    to_scalar.wait()

    def gathered(buf, r, g):
        parts = []
        for j in range(named):
            slot = slot_s[j, r]
            parts.append(buf[slot // half, lax.rem(slot, half), pl.ds(g * block, block), :])
        return jnp.concatenate(parts, axis=0)

    def prior_unit(r):
        for g in range(key_heads):
            s = lax.dot_general(
                query_rows(r, g), gathered(kbuf, r, g), NT, preferred_element_type=F32
            )
            s = [x * factor for x in columns(s)]
            before = top[r, g]
            m = jnp.maximum(before, wide_max(s))
            p = [jnp.exp2(x - m) for x in s]
            shrink = jnp.exp2(before - m)
            l = functools.reduce(jnp.add, p, tot[r, g] * shrink)
            l = 1.0 / jnp.broadcast_to(jnp.sum(l, axis=1, keepdims=True), l.shape)
            prob[r, g] = jnp.concatenate(p, axis=1).astype(BF16)
            tot[r, g] = l
            acc[r, g] = acc[r, g] * (shrink * l)

    late = [lambda: line_event(outer - 1, V)]
    if crossing:
        late = [lambda: cross_event(1, 0, V)] + late
        late += [lambda t=t: cross_event(1, t, V) for t in range(1, outer)]
    for r in range(requests):
        prior_unit(r)
        if late and r % 2 == 0 or len(late) > 3:
            late.pop(0)()
    while late:
        late.pop(0)()
    if inner > 2:
        pl.loop(2, inner)(lambda u: far(u, V))
    whole_wait(2, 1 - core, core_recv.at[2])

    for r in range(requests):
        for g in range(key_heads):
            o = jnp.dot(prob[r, g], gathered(vbuf, r, g), preferred_element_type=F32)
            o = (acc[r, g] + o * tot[r, g]).astype(BF16)
            out_ref[r, :, pl.ds(g * group, group), :] = o.reshape(steps, group, width)

    for condition, copy in pending:

        @pl.when(condition)
        def _(copy=copy):
            copy.wait_send()

    if inner > 1:
        def drain(u):
            for t in range(outer):
                for condition, a in order(t):
                    cross_wait(u, a, condition, (0, 1, 2))

        if inner > 2:
            pl.loop(1, inner)(drain)
    for kind in range(3):
        whole_wait(kind, core, core_send.at[kind])


def per_device(
    loop,
    queries,
    new_keys,
    new_values,
    suffix_keys,
    suffix_values,
    suffix_len,
    prefix_keys,
    prefix_values,
    block_ids,
    block_lists,
):
    outer, inner = fold_of(loop)
    requests, steps, head_count, width = queries.shape
    key_heads = new_keys.shape[2]
    suffix = suffix_keys.shape[1]
    block = prefix_keys.shape[1]
    named = block_lists.shape[1]
    rows = steps * head_count // key_heads
    half = outer * inner
    padded = -(-requests * steps // width) * width
    vmem = pl.BlockSpec(memory_space=pltpu.VMEM)
    smem = pl.BlockSpec(memory_space=pltpu.SMEM)
    anywhere = pl.BlockSpec(memory_space=pltpu.HBM)
    kernel = functools.partial(attend_kernel, outer, inner)
    return pl.pallas_call(
        kernel,
        out_shape=pltpu.VMEM(queries.shape, queries.dtype),
        in_specs=[anywhere] * 8 + [smem, anywhere],
        out_specs=vmem,
        scratch_shapes=[
            pltpu.VMEM((requests * steps * key_heads, width), BF16),
            pltpu.VMEM((requests * steps * key_heads, width), BF16),
            pltpu.VMEM((block * key_heads, width), BF16),
            pltpu.VMEM((block * key_heads, width), BF16),
            pltpu.VMEM((named, requests), jnp.int32),
            pltpu.SMEM((requests,), jnp.int32),
            pltpu.VMEM((key_heads, padded, width), BF16),
            pltpu.VMEM((key_heads, padded, width), BF16),
            pltpu.VMEM(queries.shape, BF16),
            pltpu.VMEM((requests, suffix * key_heads, width), BF16),
            pltpu.VMEM((requests, suffix * key_heads, width), BF16),
            pltpu.VMEM((2, max(suffix, block, requests * steps) * key_heads, width), F32),
            pltpu.VMEM((2, half, key_heads * block, width), BF16),
            pltpu.VMEM((2, half, key_heads * block, width), BF16),
            pltpu.VMEM((2, half, 8, width), jnp.int32),
            pltpu.VMEM((8, 128), jnp.int32),
            pltpu.SMEM((8, 128), jnp.int32),
            pltpu.VMEM((requests, key_heads, rows, width), F32),
            pltpu.VMEM((requests, key_heads, rows, width), F32),
            pltpu.VMEM((requests, key_heads, rows, width), F32),
            pltpu.VMEM((requests, key_heads, rows, named * block), BF16),
            pltpu.SemaphoreType.DMA((1 + 2 * requests,)),
            pltpu.SemaphoreType.DMA((6,)),
            pltpu.SemaphoreType.DMA((3, half)),
            pltpu.SemaphoreType.DMA((3,)),
            pltpu.SemaphoreType.DMA((3, 2, outer)),
            pltpu.SemaphoreType.DMA((3, 2, half)),
            pltpu.SemaphoreType.DMA((3,)),
        ],
        compiler_params=pltpu.CompilerParams(
            collective_id=0, has_side_effects=True, vmem_limit_bytes=60 * 1024 * 1024
        ),
        name="attend",
    )(
        queries,
        new_keys.reshape(-1, width),
        new_values.reshape(-1, width),
        suffix_keys.reshape(requests, suffix * key_heads, width),
        suffix_values.reshape(requests, suffix * key_heads, width),
        suffix_len,
        prefix_keys.reshape(-1, width),
        prefix_values.reshape(-1, width),
        block_ids,
        block_lists.T,
    )


def solution(mesh):
    lead = ("groups", "loop")
    in_specs = (
        P(lead, None, None, None),
        P(lead, None, None, None),
        P(lead, None, None, None),
        P(lead, None, None, None),
        P(lead, None, None, None),
        P(lead),
        P(lead, None, None, None),
        P(lead, None, None, None),
        P(lead),
        P(lead, None),
    )
    return jax.shard_map(
        functools.partial(per_device, mesh.shape["loop"]),
        mesh=mesh,
        in_specs=in_specs,
        out_specs=P(lead, None, None, None),
        check_vma=False,
    )
```

```python
import functools
import math

import jax
import jax.numpy as jnp
from jax import lax
from jax.experimental import pallas as pl
from jax.experimental.pallas import tpu as pltpu
from jax.sharding import PartitionSpec as P

F32 = jnp.float32
BF16 = jnp.bfloat16
NT = (((1,), (1,)), ((), ()))


def fold_of(count):
    chips = count // 2
    inner = 1 << ((chips.bit_length() - 1) // 2)
    return chips // inner, inner


def attend_kernel(
    outer,
    inner,
    q_hbm,
    fk_hbm,
    fv_hbm,
    sk_hbm,
    sv_hbm,
    len_hbm,
    pk_hbm,
    pv_hbm,
    id_ref,
    lists_hbm,
    out_ref,
    fk_ref,
    fv_ref,
    pk_ref,
    pv_ref,
    lists_ref,
    len_ref,
    fresh_k,
    fresh_v,
    q_ref,
    sk_ref,
    sv_ref,
    wide,
    kbuf,
    vbuf,
    ibuf,
    slot_v,
    slot_s,
    top,
    tot,
    acc,
    prob,
    load_sem,
    small_sem,
    line_recv,
    core_recv,
    a_send,
    b_send,
    core_send,
):
    requests, steps, head_count, width = q_ref.shape

    key_heads = fk_ref.shape[0] // (requests * steps)
    block = pk_ref.shape[0] // key_heads
    group = head_count // key_heads
    rows = steps * group
    suffix = sk_ref.shape[1] // key_heads
    named = lists_ref.shape[0]
    factor = math.log2(math.e) / math.sqrt(width)
    bufs = (kbuf, ibuf, vbuf)

    me = lax.axis_index("loop")
    core = lax.rem(me, 2)
    chip = me // 2
    pa = chip // inner
    pb = lax.rem(chip, inner)

    def device(a, b, c):
        return {"loop": (a * inner + b) * 2 + c}

    pairs = (
        (fk_hbm, fk_ref),
        (fv_hbm, fv_ref),
        (pk_hbm, pk_ref),
        (pv_hbm, pv_ref),
        (lists_hbm, lists_ref),
        (len_hbm, len_ref),
    )
    small = [pltpu.make_async_copy(a, b, small_sem.at[i]) for i, (a, b) in enumerate(pairs)]
    for i in (2, 3, 0, 1, 5, 4):
        small[i].start()
    loads = [pltpu.make_async_copy(q_hbm, q_ref, load_sem.at[0])]
    for r in range(requests):
        loads.append(pltpu.make_async_copy(sk_hbm.at[r], sk_ref.at[r], load_sem.at[1 + 2 * r]))
        loads.append(pltpu.make_async_copy(sv_hbm.at[r], sv_ref.at[r], load_sem.at[2 + 2 * r]))
    for copy in loads:
        copy.start()

    direct = outer <= 4
    reach = outer if direct else 2
    neighbours = [(pa >= d, (pa - d, pb, core)) for d in range(1, reach)]
    neighbours += [(pa + d < outer, (pa + d, pb, core)) for d in range(1, reach)]
    neighbours += [
        (pb > 0, (pa, pb - 1, core)),
        (pb < inner - 1, (pa, pb + 1, core)),
    ]
    barrier = pltpu.get_barrier_semaphore()
    count = jnp.int32(1)
    pl.semaphore_signal(
        barrier, inc=1, device_id=device(pa, pb, 1 - core), device_id_type=pl.DeviceIdType.MESH
    )
    for there, where in neighbours:
        count = count + there.astype(jnp.int32)

        @pl.when(there)
        def _(where=where):
            pl.semaphore_signal(
                barrier, inc=1, device_id=device(*where), device_id_type=pl.DeviceIdType.MESH
            )

    def split_rows(source, area, per_head, heads=None):
        size = per_head * key_heads
        if heads is None or heads[0] == 0:
            wide[area, pl.ds(0, size), :] = source[...].astype(F32)
        return [
            wide[area, pl.ds(g, per_head, stride=key_heads), :].astype(BF16)
            for g in (heads or range(key_heads))
        ]

    mine = pa * inner + pb
    for area, (source, target) in enumerate(((pk_ref, kbuf), (pv_ref, vbuf))):
        small[2 + area].wait()
        parts = split_rows(source, area, block)
        for g in range(key_heads):
            target[core, mine, pl.ds(g * block, block), :] = parts[g]
    ibuf[core, mine] = jnp.full(ibuf.shape[2:], id_ref[0], jnp.int32)


    pending = []

    def send(kind, a, b, sem, recv, condition, where):
        copy = pltpu.make_async_remote_copy(
            src_ref=bufs[kind].at[core, a * inner + b],
            dst_ref=bufs[kind].at[core, a * inner + b],
            send_sem=sem,
            recv_sem=recv,
            device_id=device(*where),
            device_id_type=pl.DeviceIdType.MESH,
        )

        @pl.when(condition)
        def _():
            copy.start()

        return condition, copy

    def send_a(kind, a, condition, up):
        where = (pa + 1, pb, core) if up else (pa - 1, pb, core)
        ok = condition & ((pa < outer - 1) if up else (pa > 0))
        slot = a * inner + pb
        pending.append(
            send(kind, a, pb, a_send.at[kind, int(up) + 1, a], line_recv.at[kind, slot], ok, where)
        )

    def send_b(kind, a, b, condition, up, keep=True):
        where = (pa, pb + 1, core) if up else (pa, pb - 1, core)
        ok = condition & ((pb < inner - 1) if up else (pb > 0))
        slot = a * inner + b
        entry = send(kind, a, b, b_send.at[kind, int(up), slot], line_recv.at[kind, slot], ok, where)
        if keep:
            pending.append(entry)
        return entry

    def send_core(kind, a, b, condition):
        send(
            kind, a, b, core_send.at[kind], core_recv.at[kind], condition, (pa, pb, 1 - core)
        )

    def arrived(kind, a, b, condition):
        slot = a * inner + b

        @pl.when(condition)
        def _():
            here = bufs[kind].at[core, slot]
            pltpu.make_async_copy(here, here, line_recv.at[kind, slot]).wait()

    always = pa >= 0

    def own(kinds):
        for kind in kinds:
            for d in range(1, reach):
                for ok, a in ((pa + d < outer, pa + d), (pa >= d, pa - d)):
                    slot = jnp.clip(a, 0, outer - 1)
                    pending.append(
                        send(
                            kind,
                            pa,
                            pb,
                            a_send.at[kind, 0, slot],
                            line_recv.at[kind, mine],
                            ok,
                            (a, pb, core),
                        )
                    )
            send_b(kind, pa, pb, always, True)
            send_b(kind, pa, pb, always, False)
        for kind in kinds:
            send_core(kind, pa, pb, always)

    def line_event(t, kinds):
        for up, condition, a in ((True, pa >= t, pa - t), (False, pa + t < outer, pa + t)):
            a = jnp.clip(a, 0, outer - 1)
            for kind in kinds:
                arrived(kind, a, pb, condition)
                if not direct:
                    send_a(kind, a, condition, up)
                send_b(kind, a, pb, condition, True)
                send_b(kind, a, pb, condition, False)
                send_core(kind, a, pb, condition)

    def cross_one(u, a, condition, kinds):
        for up, here, b in ((True, pb >= u, pb - u), (False, pb + u < inner, pb + u)):
            here = here & condition
            b = jnp.clip(b, 0, inner - 1)
            for kind in kinds:
                arrived(kind, a, b, here)
                send_b(kind, a, b, here, up, keep=False)
                send_core(kind, a, b, here)

    def cross_wait(u, a, condition, kinds):
        for up, here, b in ((True, pb >= u, pb - u), (False, pb + u < inner, pb + u)):
            ok = here & condition & ((pb < inner - 1) if up else (pb > 0))
            slot = a * inner + jnp.clip(b, 0, inner - 1)
            for kind in kinds:

                @pl.when(ok)
                def _(kind=kind, slot=slot, up=up):
                    piece = bufs[kind].at[core, slot]
                    pltpu.make_async_copy(piece, piece, b_send.at[kind, int(up), slot]).wait()

    def order(t):
        if t == 0:
            return [(always, pa)]
        return [
            (pa >= t, jnp.clip(pa - t, 0, outer - 1)),
            (pa + t < outer, jnp.clip(pa + t, 0, outer - 1)),
        ]

    def cross_event(u, t, kinds):
        for condition, a in order(t):
            cross_one(u, a, condition, kinds)

    def query_rows(r, g):
        return q_ref[r, :, pl.ds(g * group, group), :].reshape(rows, width)

    def wide_max(parts):
        best = functools.reduce(jnp.maximum, parts)
        return jnp.broadcast_to(jnp.max(best, axis=1, keepdims=True), best.shape)

    def columns(x):
        return [x[:, i : i + width] for i in range(0, x.shape[1], width)]

    def fresh_unit():
        fresh = requests * steps
        small[0].wait()
        small[1].wait()
        keys = split_rows(fk_ref, 0, fresh)
        values = split_rows(fv_ref, 1, fresh)
        for part, held in ((keys, fresh_k), (values, fresh_v)):
            held[...] = jnp.zeros_like(held)
            for g in range(key_heads):
                held[g, pl.ds(0, fresh), :] = part[g]
        loads[0].wait()
        small[5].wait()

    def suffix_unit(r, heads):
        loads[1 + 2 * r].wait() if heads[0] == 0 else None
        keys = split_rows(sk_ref.at[r], 0, suffix, heads)
        loads[2 + 2 * r].wait() if heads[0] == 0 else None
        values = split_rows(sv_ref.at[r], 1, suffix, heads)
        slot = lax.broadcasted_iota(jnp.int32, (8, suffix), 1)
        hidden = jnp.where(slot < len_ref[r], 0.0, -jnp.inf)
        hidden = jnp.concatenate([hidden] * (rows // 8), axis=0)
        row = lax.broadcasted_iota(jnp.int32, (rows, fresh_k.shape[1]), 0)
        col = lax.broadcasted_iota(jnp.int32, (rows, fresh_k.shape[1]), 1) - r * steps
        own_hidden = jnp.where((col >= 0) & (col <= row // group), 0.0, -jnp.inf)
        biases = columns(hidden) + columns(own_hidden)
        held = [(fresh_k[g], fresh_v[g]) for g in heads]
        s = [
            lax.dot_general(
                query_rows(r, g),
                jnp.concatenate([k, more[0]], axis=0),
                NT,
                preferred_element_type=F32,
            )
            for g, k, more in zip(heads, keys, held)
        ]
        s = [[x * factor + bias for x, bias in zip(columns(x), biases)] for x in s]
        m = [wide_max(x) for x in s]
        p = [[jnp.exp2(x - most) for x in part] for part, most in zip(s, m)]
        o = [
            jnp.dot(
                jnp.concatenate(part, axis=1).astype(BF16),
                jnp.concatenate([v, more[1]], axis=0),
                preferred_element_type=F32,
            )
            for part, v, more in zip(p, values, held)
        ]
        for i, g in enumerate(heads):
            top[r, g] = m[i]
            tot[r, g] = functools.reduce(jnp.add, p[i])
            acc[r, g] = o[i]

    K = (0, 1)
    V = (2,)
    crossing = inner > 1
    halves = [tuple(range(g, min(g + 2, key_heads))) for g in range(0, key_heads, 2)]
    units = [functools.partial(suffix_unit, r, heads) for r in range(requests) for heads in halves]
    early = [(5, lambda: line_event(1, K))]
    if crossing:
        early.append((6, lambda: cross_event(1, 0, K)))
    early.append((8, lambda: line_event(1, V)))
    for t in range(2, outer):
        early.append((11 + 2 * (t - 2), lambda t=t: line_event(t, K)))
        if crossing:
            early.append((13 + 2 * (t - 2), lambda t=t: cross_event(1, t - 1, K)))

    fresh_unit()
    pl.semaphore_wait(barrier, count)
    own(K)
    own(V)
    for place, unit in enumerate(units):
        unit()
        while early and early[0][0] <= place:
            early.pop(0)[1]()
    for _, event in early:
        event()
    if crossing:
        cross_event(1, outer - 1, K)

    def far(u, kinds):
        for t in range(outer):
            cross_event(u, t, kinds)

    if inner > 2:
        pl.loop(2, inner)(lambda u: far(u, K))

    def whole_wait(kind, side, sem):
        half = bufs[kind].at[side]
        pltpu.make_async_copy(half, half, sem).wait()

    whole_wait(0, 1 - core, core_recv.at[0])
    whole_wait(1, 1 - core, core_recv.at[1])

    half = outer * inner
    ids = ibuf[:, :, 0, :].reshape(2 * half, width)[:, :requests]
    place = lax.broadcasted_iota(jnp.int32, ids.shape, 0)
    small[4].wait()
    for j in range(named):
        match = ids == lists_ref[pl.ds(j, 1), :]
        slot_v[pl.ds(j, 1), pl.ds(0, requests)] = jnp.max(
            jnp.where(match, place, 0), axis=0, keepdims=True
        )
    to_scalar = pltpu.make_async_copy(slot_v, slot_s, load_sem.at[0])
    to_scalar.start()
    to_scalar.wait()

    def gathered(buf, r, g):
        parts = []
        for j in range(named):
            slot = slot_s[j, r]
            parts.append(buf[slot // half, lax.rem(slot, half), pl.ds(g * block, block), :])
        return jnp.concatenate(parts, axis=0)

    def prior_unit(r):
        heads = range(key_heads)
        s = [
            lax.dot_general(
                query_rows(r, g), gathered(kbuf, r, g), NT, preferred_element_type=F32
            )
            for g in heads
        ]
        before = [top[r, g] for g in heads]
        held = [tot[r, g] for g in heads]
        s = [[x * factor for x in columns(x)] for x in s]
        m = [jnp.maximum(b, wide_max(x)) for b, x in zip(before, s)]
        p = [[jnp.exp2(x - most) for x in part] for part, most in zip(s, m)]
        shrink = [jnp.exp2(b - most) for b, most in zip(before, m)]
        l = [functools.reduce(jnp.add, part, h * k) for part, h, k in zip(p, held, shrink)]
        l = [1.0 / jnp.broadcast_to(jnp.sum(x, axis=1, keepdims=True), x.shape) for x in l]
        for g in heads:
            prob[r, g] = jnp.concatenate(p[g], axis=1).astype(BF16)
            tot[r, g] = l[g]
            acc[r, g] = acc[r, g] * (shrink[g] * l[g])

    late = [lambda t=t: line_event(t, V) for t in range(2, outer)]
    if crossing:
        late.insert(1, lambda: cross_event(1, 0, V))
        late += [lambda t=t: cross_event(1, t, V) for t in range(1, outer)]
    for r in range(requests):
        prior_unit(r)
        if late:
            late.pop(0)()
    while late:
        late.pop(0)()
    if inner > 2:
        pl.loop(2, inner)(lambda u: far(u, V))
    whole_wait(2, 1 - core, core_recv.at[2])

    for r in range(requests):
        o = [
            jnp.dot(prob[r, g], gathered(vbuf, r, g), preferred_element_type=F32)
            for g in range(key_heads)
        ]
        for g in range(key_heads):
            done = (acc[r, g] + o[g] * tot[r, g]).astype(BF16)
            out_ref[r, :, pl.ds(g * group, group), :] = done.reshape(steps, group, width)

    for condition, copy in pending:

        @pl.when(condition)
        def _(copy=copy):
            copy.wait_send()

    if inner > 1:
        def drain(u):
            for t in range(outer):
                for condition, a in order(t):
                    cross_wait(u, a, condition, (0, 1, 2))

        if inner > 2:
            pl.loop(1, inner)(drain)
    for kind in range(3):
        whole_wait(kind, core, core_send.at[kind])


def per_device(
    loop,
    queries,
    new_keys,
    new_values,
    suffix_keys,
    suffix_values,
    suffix_len,
    prefix_keys,
    prefix_values,
    block_ids,
    block_lists,
):
    outer, inner = fold_of(loop)
    requests, steps, head_count, width = queries.shape
    key_heads = new_keys.shape[2]
    suffix = suffix_keys.shape[1]
    block = prefix_keys.shape[1]
    named = block_lists.shape[1]
    rows = steps * head_count // key_heads
    half = outer * inner
    padded = -(-requests * steps // width) * width
    vmem = pl.BlockSpec(memory_space=pltpu.VMEM)
    smem = pl.BlockSpec(memory_space=pltpu.SMEM)
    anywhere = pl.BlockSpec(memory_space=pltpu.HBM)
    kernel = functools.partial(attend_kernel, outer, inner)
    return pl.pallas_call(
        kernel,
        out_shape=pltpu.VMEM(queries.shape, queries.dtype),
        in_specs=[anywhere] * 8 + [smem, anywhere],
        out_specs=vmem,
        scratch_shapes=[
            pltpu.VMEM((requests * steps * key_heads, width), BF16),
            pltpu.VMEM((requests * steps * key_heads, width), BF16),
            pltpu.VMEM((block * key_heads, width), BF16),
            pltpu.VMEM((block * key_heads, width), BF16),
            pltpu.VMEM((named, requests), jnp.int32),
            pltpu.SMEM((requests,), jnp.int32),
            pltpu.VMEM((key_heads, padded, width), BF16),
            pltpu.VMEM((key_heads, padded, width), BF16),
            pltpu.VMEM(queries.shape, BF16),
            pltpu.VMEM((requests, suffix * key_heads, width), BF16),
            pltpu.VMEM((requests, suffix * key_heads, width), BF16),
            pltpu.VMEM((2, max(suffix, block, requests * steps) * key_heads, width), F32),
            pltpu.VMEM((2, half, key_heads * block, width), BF16),
            pltpu.VMEM((2, half, key_heads * block, width), BF16),
            pltpu.VMEM((2, half, 8, width), jnp.int32),
            pltpu.VMEM((8, 128), jnp.int32),
            pltpu.SMEM((8, 128), jnp.int32),
            pltpu.VMEM((requests, key_heads, rows, width), F32),
            pltpu.VMEM((requests, key_heads, rows, width), F32),
            pltpu.VMEM((requests, key_heads, rows, width), F32),
            pltpu.VMEM((requests, key_heads, rows, named * block), BF16),
            pltpu.SemaphoreType.DMA((1 + 2 * requests,)),
            pltpu.SemaphoreType.DMA((6,)),
            pltpu.SemaphoreType.DMA((3, half)),
            pltpu.SemaphoreType.DMA((3,)),
            pltpu.SemaphoreType.DMA((3, 3, outer)),
            pltpu.SemaphoreType.DMA((3, 2, half)),
            pltpu.SemaphoreType.DMA((3,)),
        ],
        compiler_params=pltpu.CompilerParams(
            collective_id=0, has_side_effects=True, vmem_limit_bytes=60 * 1024 * 1024
        ),
        name="attend",
    )(
        queries,
        new_keys.reshape(-1, width),
        new_values.reshape(-1, width),
        suffix_keys.reshape(requests, suffix * key_heads, width),
        suffix_values.reshape(requests, suffix * key_heads, width),
        suffix_len,
        prefix_keys.reshape(-1, width),
        prefix_values.reshape(-1, width),
        block_ids,
        block_lists.T,
    )


def solution(mesh):
    lead = ("groups", "loop")
    in_specs = (
        P(lead, None, None, None),
        P(lead, None, None, None),
        P(lead, None, None, None),
        P(lead, None, None, None),
        P(lead, None, None, None),
        P(lead),
        P(lead, None, None, None),
        P(lead, None, None, None),
        P(lead),
        P(lead, None),
    )
    return jax.shard_map(
        functools.partial(per_device, mesh.shape["loop"]),
        mesh=mesh,
        in_specs=in_specs,
        out_specs=P(lead, None, None, None),
        check_vma=False,
    )
```

```python
import functools
import math

import jax
import jax.numpy as jnp
from jax import lax
from jax.experimental import pallas as pl
from jax.experimental.pallas import tpu as pltpu
from jax.sharding import PartitionSpec as P

F32 = jnp.float32
BF16 = jnp.bfloat16
NT = (((1,), (1,)), ((), ()))


def fold_of(count):
    chips = count // 2
    inner = 1 << ((chips.bit_length() - 1) // 2)
    return chips // inner, inner


def attend_kernel(
    outer,
    inner,
    q_hbm,
    fk_hbm,
    fv_hbm,
    sk_hbm,
    sv_hbm,
    len_hbm,
    pk_hbm,
    pv_hbm,
    id_ref,
    lists_hbm,
    out_ref,
    fk_ref,
    fv_ref,
    pk_ref,
    pv_ref,
    lists_ref,
    len_ref,
    fresh_k,
    fresh_v,
    q_ref,
    sk_ref,
    sv_ref,
    wide,
    kbuf,
    vbuf,
    ibuf,
    slot_v,
    slot_s,
    top,
    tot,
    acc,
    prob,
    load_sem,
    small_sem,
    line_recv,
    core_recv,
    a_send,
    b_send,
    core_send,
):
    requests, steps, head_count, width = q_ref.shape

    key_heads = fk_ref.shape[0] // (requests * steps)
    block = pk_ref.shape[0] // key_heads
    group = head_count // key_heads
    rows = steps * group
    suffix = sk_ref.shape[1] // key_heads
    named = lists_ref.shape[0]
    factor = math.log2(math.e) / math.sqrt(width)
    bufs = (kbuf, ibuf, vbuf)

    me = lax.axis_index("loop")
    core = lax.rem(me, 2)
    chip = me // 2
    pa = chip // inner
    pb = lax.rem(chip, inner)

    def device(a, b, c):
        return {"loop": (a * inner + b) * 2 + c}

    pairs = (
        (fk_hbm, fk_ref),
        (fv_hbm, fv_ref),
        (pk_hbm, pk_ref),
        (pv_hbm, pv_ref),
        (lists_hbm, lists_ref),
        (len_hbm, len_ref),
    )
    small = [pltpu.make_async_copy(a, b, small_sem.at[i]) for i, (a, b) in enumerate(pairs)]
    for i in (2, 3, 0, 1, 5, 4):
        small[i].start()
    loads = [pltpu.make_async_copy(q_hbm, q_ref, load_sem.at[0])]
    for r in range(requests):
        loads.append(pltpu.make_async_copy(sk_hbm.at[r], sk_ref.at[r], load_sem.at[1 + 2 * r]))
        loads.append(pltpu.make_async_copy(sv_hbm.at[r], sv_ref.at[r], load_sem.at[2 + 2 * r]))
    for copy in loads:
        copy.start()

    jumps = (1, 3) if outer == 4 else (1,)
    neighbours = [(pa >= d, (pa - d, pb, core)) for d in jumps]
    neighbours += [(pa + d < outer, (pa + d, pb, core)) for d in jumps]
    neighbours += [
        (pb > 0, (pa, pb - 1, core)),
        (pb < inner - 1, (pa, pb + 1, core)),
    ]
    barrier = pltpu.get_barrier_semaphore()
    count = jnp.int32(1)
    pl.semaphore_signal(
        barrier, inc=1, device_id=device(pa, pb, 1 - core), device_id_type=pl.DeviceIdType.MESH
    )
    for there, where in neighbours:
        count = count + there.astype(jnp.int32)

        @pl.when(there)
        def _(where=where):
            pl.semaphore_signal(
                barrier, inc=1, device_id=device(*where), device_id_type=pl.DeviceIdType.MESH
            )

    def split_rows(source, area, per_head, heads=None):
        size = per_head * key_heads
        if heads is None or heads[0] == 0:
            wide[area, pl.ds(0, size), :] = source[...].astype(F32)
        return [
            wide[area, pl.ds(g, per_head, stride=key_heads), :].astype(BF16)
            for g in (heads or range(key_heads))
        ]

    mine = pa * inner + pb
    for area, (source, target) in enumerate(((pk_ref, kbuf), (pv_ref, vbuf))):
        small[2 + area].wait()
        parts = split_rows(source, area, block)
        for g in range(key_heads):
            target[core, mine, pl.ds(g * block, block), :] = parts[g]
    ibuf[core, mine] = jnp.full(ibuf.shape[2:], id_ref[0], jnp.int32)


    pending = []

    def send(kind, a, b, sem, recv, condition, where):
        copy = pltpu.make_async_remote_copy(
            src_ref=bufs[kind].at[core, a * inner + b],
            dst_ref=bufs[kind].at[core, a * inner + b],
            send_sem=sem,
            recv_sem=recv,
            device_id=device(*where),
            device_id_type=pl.DeviceIdType.MESH,
        )

        @pl.when(condition)
        def _():
            copy.start()

        return condition, copy

    def send_a(kind, a, condition, up):
        where = (pa + 1, pb, core) if up else (pa - 1, pb, core)
        ok = condition & ((pa < outer - 1) if up else (pa > 0))
        slot = a * inner + pb
        pending.append(
            send(kind, a, pb, a_send.at[kind, int(up) + 1, a], line_recv.at[kind, slot], ok, where)
        )

    def send_b(kind, a, b, condition, up, keep=True):
        where = (pa, pb + 1, core) if up else (pa, pb - 1, core)
        ok = condition & ((pb < inner - 1) if up else (pb > 0))
        slot = a * inner + b
        entry = send(kind, a, b, b_send.at[kind, int(up), slot], line_recv.at[kind, slot], ok, where)
        if keep:
            pending.append(entry)
        return entry

    def send_core(kind, a, b, condition):
        send(
            kind, a, b, core_send.at[kind], core_recv.at[kind], condition, (pa, pb, 1 - core)
        )

    def arrived(kind, a, b, condition):
        slot = a * inner + b

        @pl.when(condition)
        def _():
            here = bufs[kind].at[core, slot]
            pltpu.make_async_copy(here, here, line_recv.at[kind, slot]).wait()

    always = pa >= 0

    def own(kinds):
        for kind in kinds:
            for d in jumps if kind != 2 else (1,):
                for ok, a in ((pa + d < outer, pa + d), (pa >= d, pa - d)):
                    slot = jnp.clip(a, 0, outer - 1)
                    pending.append(
                        send(
                            kind,
                            pa,
                            pb,
                            a_send.at[kind, 0, slot],
                            line_recv.at[kind, mine],
                            ok,
                            (a, pb, core),
                        )
                    )
            send_b(kind, pa, pb, always, True)
            send_b(kind, pa, pb, always, False)
        for kind in kinds:
            send_core(kind, pa, pb, always)

    def line_event(t, kinds):
        for up, condition, a in ((True, pa >= t, pa - t), (False, pa + t < outer, pa + t)):
            a = jnp.clip(a, 0, outer - 1)
            for kind in kinds:
                arrived(kind, a, pb, condition)
                if kind == 2 or t + 1 < outer - 1 or len(jumps) == 1:
                    send_a(kind, a, condition, up)
                send_b(kind, a, pb, condition, True)
                send_b(kind, a, pb, condition, False)
                send_core(kind, a, pb, condition)

    def cross_one(u, a, condition, kinds):
        for up, here, b in ((True, pb >= u, pb - u), (False, pb + u < inner, pb + u)):
            here = here & condition
            b = jnp.clip(b, 0, inner - 1)
            for kind in kinds:
                arrived(kind, a, b, here)
                send_b(kind, a, b, here, up, keep=False)
                send_core(kind, a, b, here)

    def cross_wait(u, a, condition, kinds):
        for up, here, b in ((True, pb >= u, pb - u), (False, pb + u < inner, pb + u)):
            ok = here & condition & ((pb < inner - 1) if up else (pb > 0))
            slot = a * inner + jnp.clip(b, 0, inner - 1)
            for kind in kinds:

                @pl.when(ok)
                def _(kind=kind, slot=slot, up=up):
                    piece = bufs[kind].at[core, slot]
                    pltpu.make_async_copy(piece, piece, b_send.at[kind, int(up), slot]).wait()

    def order(t):
        if t == 0:
            return [(always, pa)]
        return [
            (pa >= t, jnp.clip(pa - t, 0, outer - 1)),
            (pa + t < outer, jnp.clip(pa + t, 0, outer - 1)),
        ]

    def cross_event(u, t, kinds):
        for condition, a in order(t):
            cross_one(u, a, condition, kinds)

    def query_rows(r, g):
        return q_ref[r, :, pl.ds(g * group, group), :].reshape(rows, width)

    def wide_max(parts):
        best = functools.reduce(jnp.maximum, parts)
        return jnp.broadcast_to(jnp.max(best, axis=1, keepdims=True), best.shape)

    def columns(x):
        return [x[:, i : i + width] for i in range(0, x.shape[1], width)]

    def fresh_unit():
        fresh = requests * steps
        small[0].wait()
        small[1].wait()
        keys = split_rows(fk_ref, 0, fresh)
        values = split_rows(fv_ref, 1, fresh)
        for part, held in ((keys, fresh_k), (values, fresh_v)):
            held[...] = jnp.zeros_like(held)
            for g in range(key_heads):
                held[g, pl.ds(0, fresh), :] = part[g]
        loads[0].wait()
        small[5].wait()

    def suffix_unit(r, heads):
        loads[1 + 2 * r].wait() if heads[0] == 0 else None
        keys = split_rows(sk_ref.at[r], 0, suffix, heads)
        loads[2 + 2 * r].wait() if heads[0] == 0 else None
        values = split_rows(sv_ref.at[r], 1, suffix, heads)
        slot = lax.broadcasted_iota(jnp.int32, (8, suffix), 1)
        hidden = jnp.where(slot < len_ref[r], 0.0, -jnp.inf)
        hidden = jnp.concatenate([hidden] * (rows // 8), axis=0)
        row = lax.broadcasted_iota(jnp.int32, (rows, fresh_k.shape[1]), 0)
        col = lax.broadcasted_iota(jnp.int32, (rows, fresh_k.shape[1]), 1) - r * steps
        own_hidden = jnp.where((col >= 0) & (col <= row // group), 0.0, -jnp.inf)
        biases = columns(hidden) + columns(own_hidden)
        held = [(fresh_k[g], fresh_v[g]) for g in heads]
        s = [
            lax.dot_general(
                query_rows(r, g),
                jnp.concatenate([k, more[0]], axis=0),
                NT,
                preferred_element_type=F32,
            )
            for g, k, more in zip(heads, keys, held)
        ]
        s = [[x * factor + bias for x, bias in zip(columns(x), biases)] for x in s]
        m = [wide_max(x) for x in s]
        p = [[jnp.exp2(x - most) for x in part] for part, most in zip(s, m)]
        o = [
            jnp.dot(
                jnp.concatenate(part, axis=1).astype(BF16),
                jnp.concatenate([v, more[1]], axis=0),
                preferred_element_type=F32,
            )
            for part, v, more in zip(p, values, held)
        ]
        for i, g in enumerate(heads):
            top[r, g] = m[i]
            tot[r, g] = functools.reduce(jnp.add, p[i])
            acc[r, g] = o[i]

    K = (0, 1)
    V = (2,)
    crossing = inner > 1
    halves = [tuple(range(g, min(g + 2, key_heads))) for g in range(0, key_heads, 2)]
    units = [functools.partial(suffix_unit, r, heads) for r in range(requests) for heads in halves]
    early = [(1, lambda: (line_event(1, K), own(V)))]
    for t in range(2, outer):
        early.append((4 * t - 4 + (t > 2) * 2, lambda t=t: line_event(t, K)))
        early.append((4 * t + (t > 2), lambda t=t: line_event(t - 1, V)))
    if crossing:
        early.append((3, lambda: cross_event(1, 0, K)))
        for t in range(1, outer - 1):
            early.append((3 + 4 * t, lambda t=t: cross_event(1, t, K)))
    early.sort(key=lambda entry: entry[0])

    fresh_unit()
    pl.semaphore_wait(barrier, count)
    own(K)
    for place, unit in enumerate(units):
        unit()
        while early and early[0][0] <= place:
            early.pop(0)[1]()
    for _, event in early:
        event()
    if crossing:
        cross_event(1, outer - 1, K)

    def far(u, kinds):
        for t in range(outer):
            cross_event(u, t, kinds)

    if inner > 2:
        pl.loop(2, inner)(lambda u: far(u, K))

    def whole_wait(kind, side, sem):
        half = bufs[kind].at[side]
        pltpu.make_async_copy(half, half, sem).wait()

    whole_wait(0, 1 - core, core_recv.at[0])
    whole_wait(1, 1 - core, core_recv.at[1])

    half = outer * inner
    ids = ibuf[:, :, 0, :].reshape(2 * half, width)[:, :requests]
    place = lax.broadcasted_iota(jnp.int32, ids.shape, 0)
    small[4].wait()
    for j in range(named):
        match = ids == lists_ref[pl.ds(j, 1), :]
        slot_v[pl.ds(j, 1), pl.ds(0, requests)] = jnp.max(
            jnp.where(match, place, 0), axis=0, keepdims=True
        )
    to_scalar = pltpu.make_async_copy(slot_v, slot_s, load_sem.at[0])
    to_scalar.start()
    to_scalar.wait()

    def gathered(buf, r, g):
        parts = []
        for j in range(named):
            slot = slot_s[j, r]
            parts.append(buf[slot // half, lax.rem(slot, half), pl.ds(g * block, block), :])
        return jnp.concatenate(parts, axis=0)

    def prior_unit(r):
        heads = range(key_heads)
        s = [
            lax.dot_general(
                query_rows(r, g), gathered(kbuf, r, g), NT, preferred_element_type=F32
            )
            for g in heads
        ]
        before = [top[r, g] for g in heads]
        held = [tot[r, g] for g in heads]
        s = [[x * factor for x in columns(x)] for x in s]
        m = [jnp.maximum(b, wide_max(x)) for b, x in zip(before, s)]
        p = [[jnp.exp2(x - most) for x in part] for part, most in zip(s, m)]
        shrink = [jnp.exp2(b - most) for b, most in zip(before, m)]
        l = [functools.reduce(jnp.add, part, h * k) for part, h, k in zip(p, held, shrink)]
        l = [1.0 / jnp.broadcast_to(jnp.sum(x, axis=1, keepdims=True), x.shape) for x in l]
        for g in heads:
            prob[r, g] = jnp.concatenate(p[g], axis=1).astype(BF16)
            tot[r, g] = l[g]
            acc[r, g] = acc[r, g] * (shrink[g] * l[g])

    late = [lambda: line_event(outer - 1, V)]
    if crossing:
        late.insert(1, lambda: cross_event(1, 0, V))
        late += [lambda t=t: cross_event(1, t, V) for t in range(1, outer)]
    for r in range(requests):
        prior_unit(r)
        if late:
            late.pop(0)()
    while late:
        late.pop(0)()
    if inner > 2:
        pl.loop(2, inner)(lambda u: far(u, V))
    whole_wait(2, 1 - core, core_recv.at[2])

    for r in range(requests):
        o = [
            jnp.dot(prob[r, g], gathered(vbuf, r, g), preferred_element_type=F32)
            for g in range(key_heads)
        ]
        for g in range(key_heads):
            done = (acc[r, g] + o[g] * tot[r, g]).astype(BF16)
            out_ref[r, :, pl.ds(g * group, group), :] = done.reshape(steps, group, width)

    for condition, copy in pending:

        @pl.when(condition)
        def _(copy=copy):
            copy.wait_send()

    if inner > 1:
        def drain(u):
            for t in range(outer):
                for condition, a in order(t):
                    cross_wait(u, a, condition, (0, 1, 2))

        if inner > 2:
            pl.loop(1, inner)(drain)
    for kind in range(3):
        whole_wait(kind, core, core_send.at[kind])


def per_device(
    loop,
    queries,
    new_keys,
    new_values,
    suffix_keys,
    suffix_values,
    suffix_len,
    prefix_keys,
    prefix_values,
    block_ids,
    block_lists,
):
    outer, inner = fold_of(loop)
    requests, steps, head_count, width = queries.shape
    key_heads = new_keys.shape[2]
    suffix = suffix_keys.shape[1]
    block = prefix_keys.shape[1]
    named = block_lists.shape[1]
    rows = steps * head_count // key_heads
    half = outer * inner
    padded = -(-requests * steps // width) * width
    vmem = pl.BlockSpec(memory_space=pltpu.VMEM)
    smem = pl.BlockSpec(memory_space=pltpu.SMEM)
    anywhere = pl.BlockSpec(memory_space=pltpu.HBM)
    kernel = functools.partial(attend_kernel, outer, inner)
    return pl.pallas_call(
        kernel,
        out_shape=pltpu.VMEM(queries.shape, queries.dtype),
        in_specs=[anywhere] * 8 + [smem, anywhere],
        out_specs=vmem,
        scratch_shapes=[
            pltpu.VMEM((requests * steps * key_heads, width), BF16),
            pltpu.VMEM((requests * steps * key_heads, width), BF16),
            pltpu.VMEM((block * key_heads, width), BF16),
            pltpu.VMEM((block * key_heads, width), BF16),
            pltpu.VMEM((named, requests), jnp.int32),
            pltpu.SMEM((requests,), jnp.int32),
            pltpu.VMEM((key_heads, padded, width), BF16),
            pltpu.VMEM((key_heads, padded, width), BF16),
            pltpu.VMEM(queries.shape, BF16),
            pltpu.VMEM((requests, suffix * key_heads, width), BF16),
            pltpu.VMEM((requests, suffix * key_heads, width), BF16),
            pltpu.VMEM((2, max(suffix, block, requests * steps) * key_heads, width), F32),
            pltpu.VMEM((2, half, key_heads * block, width), BF16),
            pltpu.VMEM((2, half, key_heads * block, width), BF16),
            pltpu.VMEM((2, half, 8, width), jnp.int32),
            pltpu.VMEM((8, 128), jnp.int32),
            pltpu.SMEM((8, 128), jnp.int32),
            pltpu.VMEM((requests, key_heads, rows, width), F32),
            pltpu.VMEM((requests, key_heads, rows, width), F32),
            pltpu.VMEM((requests, key_heads, rows, width), F32),
            pltpu.VMEM((requests, key_heads, rows, named * block), BF16),
            pltpu.SemaphoreType.DMA((1 + 2 * requests,)),
            pltpu.SemaphoreType.DMA((6,)),
            pltpu.SemaphoreType.DMA((3, half)),
            pltpu.SemaphoreType.DMA((3,)),
            pltpu.SemaphoreType.DMA((3, 3, outer)),
            pltpu.SemaphoreType.DMA((3, 2, half)),
            pltpu.SemaphoreType.DMA((3,)),
        ],
        compiler_params=pltpu.CompilerParams(
            collective_id=0, has_side_effects=True, vmem_limit_bytes=60 * 1024 * 1024
        ),
        name="attend",
    )(
        queries,
        new_keys.reshape(-1, width),
        new_values.reshape(-1, width),
        suffix_keys.reshape(requests, suffix * key_heads, width),
        suffix_values.reshape(requests, suffix * key_heads, width),
        suffix_len,
        prefix_keys.reshape(-1, width),
        prefix_values.reshape(-1, width),
        block_ids,
        block_lists.T,
    )


def solution(mesh):
    lead = ("groups", "loop")
    in_specs = (
        P(lead, None, None, None),
        P(lead, None, None, None),
        P(lead, None, None, None),
        P(lead, None, None, None),
        P(lead, None, None, None),
        P(lead),
        P(lead, None, None, None),
        P(lead, None, None, None),
        P(lead),
        P(lead, None),
    )
    return jax.shard_map(
        functools.partial(per_device, mesh.shape["loop"]),
        mesh=mesh,
        in_specs=in_specs,
        out_specs=P(lead, None, None, None),
        check_vma=False,
    )
```

```python
import functools
import math

import jax
import jax.numpy as jnp
from jax import lax
from jax.experimental import pallas as pl
from jax.experimental.pallas import tpu as pltpu
from jax.sharding import PartitionSpec as P

F32 = jnp.float32
BF16 = jnp.bfloat16
NT = (((1,), (1,)), ((), ()))


def fold_of(count):
    chips = count // 2
    inner = 1 << ((chips.bit_length() - 1) // 2)
    return chips // inner, inner


def attend_kernel(
    outer,
    inner,
    q_hbm,
    fk_hbm,
    fv_hbm,
    sk_hbm,
    sv_hbm,
    len_hbm,
    pk_hbm,
    pv_hbm,
    id_ref,
    lists_hbm,
    out_ref,
    fk_ref,
    fv_ref,
    pk_ref,
    pv_ref,
    lists_ref,
    len_ref,
    fresh_k,
    fresh_v,
    q_ref,
    sk_ref,
    sv_ref,
    wide,
    kbuf,
    vbuf,
    ibuf,
    slot_v,
    slot_s,
    top,
    tot,
    acc,
    prob,
    load_sem,
    small_sem,
    line_recv,
    core_recv,
    a_send,
    b_send,
    core_send,
):
    requests, steps, head_count, width = q_ref.shape

    key_heads = fk_ref.shape[0] // (requests * steps)
    block = pk_ref.shape[0] // key_heads
    group = head_count // key_heads
    rows = steps * group
    suffix = sk_ref.shape[1] // key_heads
    named = lists_ref.shape[0]
    factor = math.log2(math.e) / math.sqrt(width)
    bufs = (kbuf, ibuf, vbuf)

    me = lax.axis_index("loop")
    core = lax.rem(me, 2)
    chip = me // 2
    pa = chip // inner
    pb = lax.rem(chip, inner)

    def device(a, b, c):
        return {"loop": (a * inner + b) * 2 + c}

    pairs = (
        (fk_hbm, fk_ref),
        (fv_hbm, fv_ref),
        (pk_hbm, pk_ref),
        (pv_hbm, pv_ref),
        (lists_hbm, lists_ref),
        (len_hbm, len_ref),
    )
    small = [pltpu.make_async_copy(a, b, small_sem.at[i]) for i, (a, b) in enumerate(pairs)]
    for i in (2, 3, 0, 1, 5, 4):
        small[i].start()
    loads = [pltpu.make_async_copy(q_hbm, q_ref, load_sem.at[0])]
    for r in range(requests):
        loads.append(pltpu.make_async_copy(sk_hbm.at[r], sk_ref.at[r], load_sem.at[1 + 2 * r]))
        loads.append(pltpu.make_async_copy(sv_hbm.at[r], sv_ref.at[r], load_sem.at[2 + 2 * r]))
    for copy in loads:
        copy.start()

    neighbours = [(pa >= 1, (pa - 1, pb, core)), (pa + 1 < outer, (pa + 1, pb, core))]
    neighbours += [
        (pb > 0, (pa, pb - 1, core)),
        (pb < inner - 1, (pa, pb + 1, core)),
    ]
    barrier = pltpu.get_barrier_semaphore()
    count = jnp.int32(1)
    pl.semaphore_signal(
        barrier, inc=1, device_id=device(pa, pb, 1 - core), device_id_type=pl.DeviceIdType.MESH
    )
    for there, where in neighbours:
        count = count + there.astype(jnp.int32)

        @pl.when(there)
        def _(where=where):
            pl.semaphore_signal(
                barrier, inc=1, device_id=device(*where), device_id_type=pl.DeviceIdType.MESH
            )

    def split_rows(source, area, per_head, heads=None):
        size = per_head * key_heads
        if heads is None or heads[0] == 0:
            wide[area, pl.ds(0, size), :] = source[...].astype(F32)
        return [
            wide[area, pl.ds(g, per_head, stride=key_heads), :].astype(BF16)
            for g in (heads or range(key_heads))
        ]

    mine = pa * inner + pb
    for area, (source, target) in enumerate(((pk_ref, kbuf), (pv_ref, vbuf))):
        small[2 + area].wait()
        parts = split_rows(source, area, block)
        for g in range(key_heads):
            target[core, mine, pl.ds(g * block, block), :] = parts[g]
    ibuf[core, mine] = jnp.full(ibuf.shape[2:], id_ref[0], jnp.int32)


    pending = []

    def send(kind, a, b, sem, recv, condition, where):
        copy = pltpu.make_async_remote_copy(
            src_ref=bufs[kind].at[core, a * inner + b],
            dst_ref=bufs[kind].at[core, a * inner + b],
            send_sem=sem,
            recv_sem=recv,
            device_id=device(*where),
            device_id_type=pl.DeviceIdType.MESH,
        )

        @pl.when(condition)
        def _():
            copy.start()

        return condition, copy

    def send_a(kind, a, condition, up):
        where = (pa + 1, pb, core) if up else (pa - 1, pb, core)
        ok = condition & ((pa < outer - 1) if up else (pa > 0))
        slot = a * inner + pb
        pending.append(
            send(kind, a, pb, a_send.at[kind, int(up) + 1, a], line_recv.at[kind, slot], ok, where)
        )

    def send_b(kind, a, b, condition, up, keep=True):
        where = (pa, pb + 1, core) if up else (pa, pb - 1, core)
        ok = condition & ((pb < inner - 1) if up else (pb > 0))
        slot = a * inner + b
        entry = send(kind, a, b, b_send.at[kind, int(up), slot], line_recv.at[kind, slot], ok, where)
        if keep:
            pending.append(entry)
        return entry

    def send_core(kind, a, b, condition):
        send(
            kind, a, b, core_send.at[kind], core_recv.at[kind], condition, (pa, pb, 1 - core)
        )

    def arrived(kind, a, b, condition):
        slot = a * inner + b

        @pl.when(condition)
        def _():
            here = bufs[kind].at[core, slot]
            pltpu.make_async_copy(here, here, line_recv.at[kind, slot]).wait()

    always = pa >= 0

    def own(kinds):
        for kind in kinds:
            for d in (1,):
                for ok, a in ((pa + d < outer, pa + d), (pa >= d, pa - d)):
                    slot = jnp.clip(a, 0, outer - 1)
                    pending.append(
                        send(
                            kind,
                            pa,
                            pb,
                            a_send.at[kind, 0, slot],
                            line_recv.at[kind, mine],
                            ok,
                            (a, pb, core),
                        )
                    )
            send_b(kind, pa, pb, always, True)
            send_b(kind, pa, pb, always, False)
        for kind in kinds:
            send_core(kind, pa, pb, always)

    def line_event(t, kinds):
        for up, condition, a in ((True, pa >= t, pa - t), (False, pa + t < outer, pa + t)):
            a = jnp.clip(a, 0, outer - 1)
            for kind in kinds:
                arrived(kind, a, pb, condition)
                send_a(kind, a, condition, up)
                send_b(kind, a, pb, condition, True)
                send_b(kind, a, pb, condition, False)
                send_core(kind, a, pb, condition)

    def cross_one(u, a, condition, kinds):
        for up, here, b in ((True, pb >= u, pb - u), (False, pb + u < inner, pb + u)):
            here = here & condition
            b = jnp.clip(b, 0, inner - 1)
            for kind in kinds:
                arrived(kind, a, b, here)
                send_b(kind, a, b, here, up, keep=False)
                send_core(kind, a, b, here)

    def cross_wait(u, a, condition, kinds):
        for up, here, b in ((True, pb >= u, pb - u), (False, pb + u < inner, pb + u)):
            ok = here & condition & ((pb < inner - 1) if up else (pb > 0))
            slot = a * inner + jnp.clip(b, 0, inner - 1)
            for kind in kinds:

                @pl.when(ok)
                def _(kind=kind, slot=slot, up=up):
                    piece = bufs[kind].at[core, slot]
                    pltpu.make_async_copy(piece, piece, b_send.at[kind, int(up), slot]).wait()

    def order(t):
        if t == 0:
            return [(always, pa)]
        return [
            (pa >= t, jnp.clip(pa - t, 0, outer - 1)),
            (pa + t < outer, jnp.clip(pa + t, 0, outer - 1)),
        ]

    def cross_event(u, t, kinds):
        for condition, a in order(t):
            cross_one(u, a, condition, kinds)

    def query_rows(r, g):
        return q_ref[r, :, pl.ds(g * group, group), :].reshape(rows, width)

    def wide_max(parts):
        best = functools.reduce(jnp.maximum, parts)
        return jnp.broadcast_to(jnp.max(best, axis=1, keepdims=True), best.shape)

    def columns(x):
        return [x[:, i : i + width] for i in range(0, x.shape[1], width)]

    def fresh_unit():
        fresh = requests * steps
        small[0].wait()
        small[1].wait()
        keys = split_rows(fk_ref, 0, fresh)
        values = split_rows(fv_ref, 1, fresh)
        for part, held in ((keys, fresh_k), (values, fresh_v)):
            held[...] = jnp.zeros_like(held)
            for g in range(key_heads):
                held[g, pl.ds(0, fresh), :] = part[g]
        loads[0].wait()
        small[5].wait()

    def suffix_unit(r, heads):
        loads[1 + 2 * r].wait() if heads[0] == 0 else None
        keys = split_rows(sk_ref.at[r], 0, suffix, heads)
        loads[2 + 2 * r].wait() if heads[0] == 0 else None
        values = split_rows(sv_ref.at[r], 1, suffix, heads)
        slot = lax.broadcasted_iota(jnp.int32, (8, suffix), 1)
        hidden = jnp.where(slot < len_ref[r], 0.0, -jnp.inf)
        hidden = jnp.concatenate([hidden] * (rows // 8), axis=0)
        row = lax.broadcasted_iota(jnp.int32, (rows, fresh_k.shape[1]), 0)
        col = lax.broadcasted_iota(jnp.int32, (rows, fresh_k.shape[1]), 1) - r * steps
        own_hidden = jnp.where((col >= 0) & (col <= row // group), 0.0, -jnp.inf)
        biases = columns(hidden) + columns(own_hidden)
        held = [(fresh_k[g], fresh_v[g]) for g in heads]
        s = [
            lax.dot_general(
                query_rows(r, g),
                jnp.concatenate([k, more[0]], axis=0),
                NT,
                preferred_element_type=F32,
            )
            for g, k, more in zip(heads, keys, held)
        ]
        s = [[x * factor + bias for x, bias in zip(columns(x), biases)] for x in s]
        m = [wide_max(x) for x in s]
        p = [[jnp.exp2(x - most) for x in part] for part, most in zip(s, m)]
        o = [
            jnp.dot(
                jnp.concatenate(part, axis=1).astype(BF16),
                jnp.concatenate([v, more[1]], axis=0),
                preferred_element_type=F32,
            )
            for part, v, more in zip(p, values, held)
        ]
        for i, g in enumerate(heads):
            top[r, g] = m[i]
            tot[r, g] = functools.reduce(jnp.add, p[i])
            acc[r, g] = o[i]

    K = (0, 1)
    V = (2,)
    crossing = inner > 1
    halves = [tuple(range(g, min(g + 2, key_heads))) for g in range(0, key_heads, 2)]
    units = [functools.partial(suffix_unit, r, heads) for r in range(requests) for heads in halves]
    early = []
    for t in range(1, outer):
        early.append((5 * t - 1 - (t > 2), lambda t=t: line_event(t, K)))
        early.append((4 * t + 3, lambda t=t: line_event(t, V)))
    if crossing:
        early.append((5, lambda: cross_event(1, 0, K)))
        early.append((12, lambda: cross_event(1, 1, K)))
    early.sort(key=lambda entry: entry[0])

    fresh_unit()
    pl.semaphore_wait(barrier, count)
    own(K)
    own(V)
    for place, unit in enumerate(units):
        unit()
        while early and early[0][0] <= place:
            early.pop(0)[1]()
    for _, event in early:
        event()
    if crossing:
        for t in range(2, outer):
            cross_event(1, t, K)

    def far(u, kinds):
        for t in range(outer):
            cross_event(u, t, kinds)

    if inner > 2:
        pl.loop(2, inner)(lambda u: far(u, K))

    def whole_wait(kind, side, sem):
        half = bufs[kind].at[side]
        pltpu.make_async_copy(half, half, sem).wait()

    whole_wait(0, 1 - core, core_recv.at[0])
    whole_wait(1, 1 - core, core_recv.at[1])

    half = outer * inner
    ids = ibuf[:, :, 0, :].reshape(2 * half, width)[:, :requests]
    place = lax.broadcasted_iota(jnp.int32, ids.shape, 0)
    small[4].wait()
    for j in range(named):
        match = ids == lists_ref[pl.ds(j, 1), :]
        slot_v[pl.ds(j, 1), pl.ds(0, requests)] = jnp.max(
            jnp.where(match, place, 0), axis=0, keepdims=True
        )
    to_scalar = pltpu.make_async_copy(slot_v, slot_s, load_sem.at[0])
    to_scalar.start()
    to_scalar.wait()

    def gathered(buf, r, g):
        parts = []
        for j in range(named):
            slot = slot_s[j, r]
            parts.append(buf[slot // half, lax.rem(slot, half), pl.ds(g * block, block), :])
        return jnp.concatenate(parts, axis=0)

    def prior_unit(r):
        heads = range(key_heads)
        s = [
            lax.dot_general(
                query_rows(r, g), gathered(kbuf, r, g), NT, preferred_element_type=F32
            )
            for g in heads
        ]
        before = [top[r, g] for g in heads]
        held = [tot[r, g] for g in heads]
        s = [[x * factor for x in columns(x)] for x in s]
        m = [jnp.maximum(b, wide_max(x)) for b, x in zip(before, s)]
        p = [[jnp.exp2(x - most) for x in part] for part, most in zip(s, m)]
        shrink = [jnp.exp2(b - most) for b, most in zip(before, m)]
        l = [functools.reduce(jnp.add, part, h * k) for part, h, k in zip(p, held, shrink)]
        l = [1.0 / jnp.broadcast_to(jnp.sum(x, axis=1, keepdims=True), x.shape) for x in l]
        for g in heads:
            prob[r, g] = jnp.concatenate(p[g], axis=1).astype(BF16)
            tot[r, g] = l[g]
            acc[r, g] = acc[r, g] * (shrink[g] * l[g])

    late = []
    if crossing:
        late = [lambda: cross_event(1, 0, V)]
        late += [lambda t=t: cross_event(1, t, V) for t in range(1, outer)]
    for r in range(requests):
        prior_unit(r)
        if late:
            late.pop(0)()
    while late:
        late.pop(0)()
    if inner > 2:
        pl.loop(2, inner)(lambda u: far(u, V))
    whole_wait(2, 1 - core, core_recv.at[2])

    for r in range(requests):
        o = [
            jnp.dot(prob[r, g], gathered(vbuf, r, g), preferred_element_type=F32)
            for g in range(key_heads)
        ]
        for g in range(key_heads):
            done = (acc[r, g] + o[g] * tot[r, g]).astype(BF16)
            out_ref[r, :, pl.ds(g * group, group), :] = done.reshape(steps, group, width)

    for condition, copy in pending:

        @pl.when(condition)
        def _(copy=copy):
            copy.wait_send()

    if inner > 1:
        def drain(u):
            for t in range(outer):
                for condition, a in order(t):
                    cross_wait(u, a, condition, (0, 1, 2))

        if inner > 2:
            pl.loop(1, inner)(drain)
    for kind in range(3):
        whole_wait(kind, core, core_send.at[kind])


def per_device(
    loop,
    queries,
    new_keys,
    new_values,
    suffix_keys,
    suffix_values,
    suffix_len,
    prefix_keys,
    prefix_values,
    block_ids,
    block_lists,
):
    outer, inner = fold_of(loop)
    requests, steps, head_count, width = queries.shape
    key_heads = new_keys.shape[2]
    suffix = suffix_keys.shape[1]
    block = prefix_keys.shape[1]
    named = block_lists.shape[1]
    rows = steps * head_count // key_heads
    half = outer * inner
    padded = -(-requests * steps // width) * width
    vmem = pl.BlockSpec(memory_space=pltpu.VMEM)
    smem = pl.BlockSpec(memory_space=pltpu.SMEM)
    anywhere = pl.BlockSpec(memory_space=pltpu.HBM)
    kernel = functools.partial(attend_kernel, outer, inner)
    return pl.pallas_call(
        kernel,
        out_shape=pltpu.VMEM(queries.shape, queries.dtype),
        in_specs=[anywhere] * 8 + [smem, anywhere],
        out_specs=vmem,
        scratch_shapes=[
            pltpu.VMEM((requests * steps * key_heads, width), BF16),
            pltpu.VMEM((requests * steps * key_heads, width), BF16),
            pltpu.VMEM((block * key_heads, width), BF16),
            pltpu.VMEM((block * key_heads, width), BF16),
            pltpu.VMEM((named, requests), jnp.int32),
            pltpu.SMEM((requests,), jnp.int32),
            pltpu.VMEM((key_heads, padded, width), BF16),
            pltpu.VMEM((key_heads, padded, width), BF16),
            pltpu.VMEM(queries.shape, BF16),
            pltpu.VMEM((requests, suffix * key_heads, width), BF16),
            pltpu.VMEM((requests, suffix * key_heads, width), BF16),
            pltpu.VMEM((2, max(suffix, block, requests * steps) * key_heads, width), F32),
            pltpu.VMEM((2, half, key_heads * block, width), BF16),
            pltpu.VMEM((2, half, key_heads * block, width), BF16),
            pltpu.VMEM((2, half, 8, width), jnp.int32),
            pltpu.VMEM((8, 128), jnp.int32),
            pltpu.SMEM((8, 128), jnp.int32),
            pltpu.VMEM((requests, key_heads, rows, width), F32),
            pltpu.VMEM((requests, key_heads, rows, width), F32),
            pltpu.VMEM((requests, key_heads, rows, width), F32),
            pltpu.VMEM((requests, key_heads, rows, named * block), BF16),
            pltpu.SemaphoreType.DMA((1 + 2 * requests,)),
            pltpu.SemaphoreType.DMA((6,)),
            pltpu.SemaphoreType.DMA((3, half)),
            pltpu.SemaphoreType.DMA((3,)),
            pltpu.SemaphoreType.DMA((3, 3, outer)),
            pltpu.SemaphoreType.DMA((3, 2, half)),
            pltpu.SemaphoreType.DMA((3,)),
        ],
        compiler_params=pltpu.CompilerParams(
            collective_id=0, has_side_effects=True, vmem_limit_bytes=60 * 1024 * 1024
        ),
        name="attend",
    )(
        queries,
        new_keys.reshape(-1, width),
        new_values.reshape(-1, width),
        suffix_keys.reshape(requests, suffix * key_heads, width),
        suffix_values.reshape(requests, suffix * key_heads, width),
        suffix_len,
        prefix_keys.reshape(-1, width),
        prefix_values.reshape(-1, width),
        block_ids,
        block_lists.T,
    )


def solution(mesh):
    lead = ("groups", "loop")
    in_specs = (
        P(lead, None, None, None),
        P(lead, None, None, None),
        P(lead, None, None, None),
        P(lead, None, None, None),
        P(lead, None, None, None),
        P(lead),
        P(lead, None, None, None),
        P(lead, None, None, None),
        P(lead),
        P(lead, None),
    )
    return jax.shard_map(
        functools.partial(per_device, mesh.shape["loop"]),
        mesh=mesh,
        in_specs=in_specs,
        out_specs=P(lead, None, None, None),
        check_vma=False,
    )
```

```python
import functools
import math

import jax
import jax.numpy as jnp
from jax import lax
from jax.experimental import pallas as pl
from jax.experimental.pallas import tpu as pltpu
from jax.sharding import PartitionSpec as P

F32 = jnp.float32
BF16 = jnp.bfloat16
NT = (((1,), (1,)), ((), ()))


def fold_of(count):
    chips = count // 2
    inner = 1 << ((chips.bit_length() - 1) // 2)
    return chips // inner, inner


def attend_kernel(
    outer,
    inner,
    q_hbm,
    fk_hbm,
    fv_hbm,
    sk_hbm,
    sv_hbm,
    len_hbm,
    pk_hbm,
    pv_hbm,
    id_ref,
    lists_hbm,
    out_ref,
    fk_ref,
    fv_ref,
    pk_ref,
    pv_ref,
    lists_ref,
    len_ref,
    fresh_k,
    fresh_v,
    q_ref,
    sk_ref,
    sv_ref,
    wide,
    kbuf,
    vbuf,
    ibuf,
    slot_v,
    slot_s,
    top,
    tot,
    acc,
    prob,
    load_sem,
    small_sem,
    line_recv,
    core_recv,
    a_send,
    b_send,
    core_send,
):
    requests, steps, head_count, width = q_ref.shape

    key_heads = fk_ref.shape[0] // (requests * steps)
    block = pk_ref.shape[0] // key_heads
    group = head_count // key_heads
    rows = steps * group
    suffix = sk_ref.shape[1] // key_heads
    named = lists_ref.shape[0]
    factor = math.log2(math.e) / math.sqrt(width)
    bufs = (kbuf, ibuf, vbuf)

    me = lax.axis_index("loop")
    core = lax.rem(me, 2)
    chip = me // 2
    pa = chip // inner
    pb = lax.rem(chip, inner)

    def device(a, b, c):
        return {"loop": (a * inner + b) * 2 + c}

    pairs = (
        (fk_hbm, fk_ref),
        (fv_hbm, fv_ref),
        (pk_hbm, pk_ref),
        (pv_hbm, pv_ref),
        (lists_hbm, lists_ref),
        (len_hbm, len_ref),
    )
    small = [pltpu.make_async_copy(a, b, small_sem.at[i]) for i, (a, b) in enumerate(pairs)]
    for i in (2, 3, 0, 1, 5, 4):
        small[i].start()
    loads = [pltpu.make_async_copy(q_hbm, q_ref, load_sem.at[0])]
    for r in range(requests):
        loads.append(pltpu.make_async_copy(sk_hbm.at[r], sk_ref.at[r], load_sem.at[1 + 2 * r]))
        loads.append(pltpu.make_async_copy(sv_hbm.at[r], sv_ref.at[r], load_sem.at[2 + 2 * r]))
    for copy in loads:
        copy.start()

    neighbours = [(pa >= 1, (pa - 1, pb, core)), (pa + 1 < outer, (pa + 1, pb, core))]
    neighbours += [
        (pb > 0, (pa, pb - 1, core)),
        (pb < inner - 1, (pa, pb + 1, core)),
    ]
    barrier = pltpu.get_barrier_semaphore()
    count = jnp.int32(1)
    pl.semaphore_signal(
        barrier, inc=1, device_id=device(pa, pb, 1 - core), device_id_type=pl.DeviceIdType.MESH
    )
    for there, where in neighbours:
        count = count + there.astype(jnp.int32)

        @pl.when(there)
        def _(where=where):
            pl.semaphore_signal(
                barrier, inc=1, device_id=device(*where), device_id_type=pl.DeviceIdType.MESH
            )

    def split_rows(source, area, per_head, heads=None):
        size = per_head * key_heads
        if heads is None or heads[0] == 0:
            wide[area, pl.ds(0, size), :] = source[...].astype(F32)
        return [
            wide[area, pl.ds(g, per_head, stride=key_heads), :].astype(BF16)
            for g in (heads or range(key_heads))
        ]

    mine = pa * inner + pb
    for area, (source, target) in enumerate(((pk_ref, kbuf), (pv_ref, vbuf))):
        small[2 + area].wait()
        parts = split_rows(source, area, block)
        for g in range(key_heads):
            target[core, mine, pl.ds(g * block, block), :] = parts[g]
    ibuf[core, mine] = jnp.full(ibuf.shape[2:], id_ref[0], jnp.int32)


    pending = []

    def send(kind, a, b, sem, recv, condition, where):
        copy = pltpu.make_async_remote_copy(
            src_ref=bufs[kind].at[core, a * inner + b],
            dst_ref=bufs[kind].at[core, a * inner + b],
            send_sem=sem,
            recv_sem=recv,
            device_id=device(*where),
            device_id_type=pl.DeviceIdType.MESH,
        )

        @pl.when(condition)
        def _():
            copy.start()

        return condition, copy

    def send_a(kind, a, condition, up):
        where = (pa + 1, pb, core) if up else (pa - 1, pb, core)
        ok = condition & ((pa < outer - 1) if up else (pa > 0))
        slot = a * inner + pb
        pending.append(
            send(kind, a, pb, a_send.at[kind, int(up) + 1, a], line_recv.at[kind, slot], ok, where)
        )

    def send_b(kind, a, b, condition, up, keep=True):
        where = (pa, pb + 1, core) if up else (pa, pb - 1, core)
        ok = condition & ((pb < inner - 1) if up else (pb > 0))
        slot = a * inner + b
        entry = send(kind, a, b, b_send.at[kind, int(up), slot], line_recv.at[kind, slot], ok, where)
        if keep:
            pending.append(entry)
        return entry

    def send_core(kind, a, b, condition):
        send(
            kind, a, b, core_send.at[kind], core_recv.at[kind], condition, (pa, pb, 1 - core)
        )

    def arrived(kind, a, b, condition):
        slot = a * inner + b

        @pl.when(condition)
        def _():
            here = bufs[kind].at[core, slot]
            pltpu.make_async_copy(here, here, line_recv.at[kind, slot]).wait()

    always = pa >= 0

    def own(kinds):
        for kind in kinds:
            for d in (1,):
                for ok, a in ((pa + d < outer, pa + d), (pa >= d, pa - d)):
                    slot = jnp.clip(a, 0, outer - 1)
                    pending.append(
                        send(
                            kind,
                            pa,
                            pb,
                            a_send.at[kind, 0, slot],
                            line_recv.at[kind, mine],
                            ok,
                            (a, pb, core),
                        )
                    )
            send_b(kind, pa, pb, always, True)
            send_b(kind, pa, pb, always, False)
        for kind in kinds:
            send_core(kind, pa, pb, always)

    def line_event(t, kinds):
        for up, condition, a in ((True, pa >= t, pa - t), (False, pa + t < outer, pa + t)):
            a = jnp.clip(a, 0, outer - 1)
            for kind in kinds:
                arrived(kind, a, pb, condition)
                send_a(kind, a, condition, up)
                send_b(kind, a, pb, condition, True)
                send_b(kind, a, pb, condition, False)
                send_core(kind, a, pb, condition)

    def cross_one(u, a, condition, kinds):
        for up, here, b in ((True, pb >= u, pb - u), (False, pb + u < inner, pb + u)):
            here = here & condition
            b = jnp.clip(b, 0, inner - 1)
            for kind in kinds:
                arrived(kind, a, b, here)
                send_b(kind, a, b, here, up, keep=False)
                send_core(kind, a, b, here)

    def cross_wait(u, a, condition, kinds):
        for up, here, b in ((True, pb >= u, pb - u), (False, pb + u < inner, pb + u)):
            ok = here & condition & ((pb < inner - 1) if up else (pb > 0))
            slot = a * inner + jnp.clip(b, 0, inner - 1)
            for kind in kinds:

                @pl.when(ok)
                def _(kind=kind, slot=slot, up=up):
                    piece = bufs[kind].at[core, slot]
                    pltpu.make_async_copy(piece, piece, b_send.at[kind, int(up), slot]).wait()

    def order(t):
        if t == 0:
            return [(always, pa)]
        return [
            (pa >= t, jnp.clip(pa - t, 0, outer - 1)),
            (pa + t < outer, jnp.clip(pa + t, 0, outer - 1)),
        ]

    def cross_event(u, t, kinds):
        for condition, a in order(t):
            cross_one(u, a, condition, kinds)

    def query_rows(r, g):
        return q_ref[r, :, pl.ds(g * group, group), :].reshape(rows, width)

    def wide_max(parts):
        best = functools.reduce(jnp.maximum, parts)
        return jnp.broadcast_to(jnp.max(best, axis=1, keepdims=True), best.shape)

    def columns(x):
        return [x[:, i : i + width] for i in range(0, x.shape[1], width)]

    def fresh_unit():
        fresh = requests * steps
        small[0].wait()
        small[1].wait()
        keys = split_rows(fk_ref, 0, fresh)
        values = split_rows(fv_ref, 1, fresh)
        for part, held in ((keys, fresh_k), (values, fresh_v)):
            held[...] = jnp.zeros_like(held)
            for g in range(key_heads):
                held[g, pl.ds(0, fresh), :] = part[g]
        loads[0].wait()
        small[5].wait()

    def suffix_unit(r, heads):
        loads[1 + 2 * r].wait() if heads[0] == 0 else None
        keys = split_rows(sk_ref.at[r], 0, suffix, heads)
        loads[2 + 2 * r].wait() if heads[0] == 0 else None
        values = split_rows(sv_ref.at[r], 1, suffix, heads)
        slot = lax.broadcasted_iota(jnp.int32, (8, suffix), 1)
        hidden = jnp.where(slot < len_ref[r], 0.0, -jnp.inf)
        hidden = jnp.concatenate([hidden] * (rows // 8), axis=0)
        row = lax.broadcasted_iota(jnp.int32, (rows, fresh_k.shape[1]), 0)
        col = lax.broadcasted_iota(jnp.int32, (rows, fresh_k.shape[1]), 1) - r * steps
        own_hidden = jnp.where((col >= 0) & (col <= row // group), 0.0, -jnp.inf)
        biases = columns(hidden) + columns(own_hidden)
        held = [(fresh_k[g], fresh_v[g]) for g in heads]
        s = [
            lax.dot_general(
                query_rows(r, g),
                jnp.concatenate([k, more[0]], axis=0),
                NT,
                preferred_element_type=F32,
            )
            for g, k, more in zip(heads, keys, held)
        ]
        s = [[x * factor + bias for x, bias in zip(columns(x), biases)] for x in s]
        m = [wide_max(x) for x in s]
        p = [[jnp.exp2(x - most) for x in part] for part, most in zip(s, m)]
        o = [
            jnp.dot(
                jnp.concatenate(part, axis=1).astype(BF16),
                jnp.concatenate([v, more[1]], axis=0),
                preferred_element_type=F32,
            )
            for part, v, more in zip(p, values, held)
        ]
        for i, g in enumerate(heads):
            top[r, g] = m[i]
            tot[r, g] = functools.reduce(jnp.add, p[i])
            acc[r, g] = o[i]

    K = (0, 1)
    V = (2,)
    crossing = inner > 1
    halves = [tuple(range(g, min(g + 2, key_heads))) for g in range(0, key_heads, 2)]
    units = [functools.partial(suffix_unit, r, heads) for r in range(requests) for heads in halves]
    early = []
    for t in range(1, outer):
        early.append((4 * t - (t > 2), lambda t=t: line_event(t, K)))
        early.append((4 * t + 2 - (t > 2), lambda t=t: line_event(t, V)))
    if crossing:
        early.append((5, lambda: cross_event(1, 0, K)))
        early.append((12, lambda: cross_event(1, 1, K)))
    early.sort(key=lambda entry: entry[0])

    fresh_unit()
    pl.semaphore_wait(barrier, count)
    own(K)
    own(V)
    for place, unit in enumerate(units):
        unit()
        while early and early[0][0] <= place:
            early.pop(0)[1]()
    for _, event in early:
        event()
    if crossing:
        for t in range(2, outer):
            cross_event(1, t, K)

    def far(u, kinds):
        for t in range(outer):
            cross_event(u, t, kinds)

    if inner > 2:
        pl.loop(2, inner)(lambda u: far(u, K))

    def whole_wait(kind, side, sem):
        half = bufs[kind].at[side]
        pltpu.make_async_copy(half, half, sem).wait()

    whole_wait(0, 1 - core, core_recv.at[0])
    whole_wait(1, 1 - core, core_recv.at[1])

    half = outer * inner
    ids = ibuf[:, :, 0, :].reshape(2 * half, width)[:, :requests]
    place = lax.broadcasted_iota(jnp.int32, ids.shape, 0)
    small[4].wait()
    for j in range(named):
        match = ids == lists_ref[pl.ds(j, 1), :]
        slot_v[pl.ds(j, 1), pl.ds(0, requests)] = jnp.max(
            jnp.where(match, place, 0), axis=0, keepdims=True
        )
    to_scalar = pltpu.make_async_copy(slot_v, slot_s, load_sem.at[0])
    to_scalar.start()
    to_scalar.wait()

    def gathered(buf, r, g):
        parts = []
        for j in range(named):
            slot = slot_s[j, r]
            parts.append(buf[slot // half, lax.rem(slot, half), pl.ds(g * block, block), :])
        return jnp.concatenate(parts, axis=0)

    def prior_unit(r):
        heads = range(key_heads)
        s = [
            lax.dot_general(
                query_rows(r, g), gathered(kbuf, r, g), NT, preferred_element_type=F32
            )
            for g in heads
        ]
        before = [top[r, g] for g in heads]
        held = [tot[r, g] for g in heads]
        s = [[x * factor for x in columns(x)] for x in s]
        m = [jnp.maximum(b, wide_max(x)) for b, x in zip(before, s)]
        p = [[jnp.exp2(x - most) for x in part] for part, most in zip(s, m)]
        shrink = [jnp.exp2(b - most) for b, most in zip(before, m)]
        l = [functools.reduce(jnp.add, part, h * k) for part, h, k in zip(p, held, shrink)]
        l = [1.0 / jnp.broadcast_to(jnp.sum(x, axis=1, keepdims=True), x.shape) for x in l]
        for g in heads:
            prob[r, g] = jnp.concatenate(p[g], axis=1).astype(BF16)
            tot[r, g] = l[g]
            acc[r, g] = acc[r, g] * (shrink[g] * l[g])

    late = []
    if crossing:
        late = [lambda: cross_event(1, 0, V)]
        late += [lambda t=t: cross_event(1, t, V) for t in range(1, outer)]
    for r in range(requests):
        prior_unit(r)
        if late:
            late.pop(0)()
    while late:
        late.pop(0)()
    if inner > 2:
        pl.loop(2, inner)(lambda u: far(u, V))
    whole_wait(2, 1 - core, core_recv.at[2])

    for r in range(requests):
        o = [
            jnp.dot(prob[r, g], gathered(vbuf, r, g), preferred_element_type=F32)
            for g in range(key_heads)
        ]
        for g in range(key_heads):
            done = (acc[r, g] + o[g] * tot[r, g]).astype(BF16)
            out_ref[r, :, pl.ds(g * group, group), :] = done.reshape(steps, group, width)

    for condition, copy in pending:

        @pl.when(condition)
        def _(copy=copy):
            copy.wait_send()

    if inner > 1:
        def drain(u):
            for t in range(outer):
                for condition, a in order(t):
                    cross_wait(u, a, condition, (0, 1, 2))

        if inner > 2:
            pl.loop(1, inner)(drain)
    for kind in range(3):
        whole_wait(kind, core, core_send.at[kind])


def per_device(
    loop,
    queries,
    new_keys,
    new_values,
    suffix_keys,
    suffix_values,
    suffix_len,
    prefix_keys,
    prefix_values,
    block_ids,
    block_lists,
):
    outer, inner = fold_of(loop)
    requests, steps, head_count, width = queries.shape
    key_heads = new_keys.shape[2]
    suffix = suffix_keys.shape[1]
    block = prefix_keys.shape[1]
    named = block_lists.shape[1]
    rows = steps * head_count // key_heads
    half = outer * inner
    padded = -(-requests * steps // width) * width
    vmem = pl.BlockSpec(memory_space=pltpu.VMEM)
    smem = pl.BlockSpec(memory_space=pltpu.SMEM)
    anywhere = pl.BlockSpec(memory_space=pltpu.HBM)
    kernel = functools.partial(attend_kernel, outer, inner)
    return pl.pallas_call(
        kernel,
        out_shape=pltpu.VMEM(queries.shape, queries.dtype),
        in_specs=[anywhere] * 8 + [smem, anywhere],
        out_specs=vmem,
        scratch_shapes=[
            pltpu.VMEM((requests * steps * key_heads, width), BF16),
            pltpu.VMEM((requests * steps * key_heads, width), BF16),
            pltpu.VMEM((block * key_heads, width), BF16),
            pltpu.VMEM((block * key_heads, width), BF16),
            pltpu.VMEM((named, requests), jnp.int32),
            pltpu.SMEM((requests,), jnp.int32),
            pltpu.VMEM((key_heads, padded, width), BF16),
            pltpu.VMEM((key_heads, padded, width), BF16),
            pltpu.VMEM(queries.shape, BF16),
            pltpu.VMEM((requests, suffix * key_heads, width), BF16),
            pltpu.VMEM((requests, suffix * key_heads, width), BF16),
            pltpu.VMEM((2, max(suffix, block, requests * steps) * key_heads, width), F32),
            pltpu.VMEM((2, half, key_heads * block, width), BF16),
            pltpu.VMEM((2, half, key_heads * block, width), BF16),
            pltpu.VMEM((2, half, 8, width), jnp.int32),
            pltpu.VMEM((8, 128), jnp.int32),
            pltpu.SMEM((8, 128), jnp.int32),
            pltpu.VMEM((requests, key_heads, rows, width), F32),
            pltpu.VMEM((requests, key_heads, rows, width), F32),
            pltpu.VMEM((requests, key_heads, rows, width), F32),
            pltpu.VMEM((requests, key_heads, rows, named * block), BF16),
            pltpu.SemaphoreType.DMA((1 + 2 * requests,)),
            pltpu.SemaphoreType.DMA((6,)),
            pltpu.SemaphoreType.DMA((3, half)),
            pltpu.SemaphoreType.DMA((3,)),
            pltpu.SemaphoreType.DMA((3, 3, outer)),
            pltpu.SemaphoreType.DMA((3, 2, half)),
            pltpu.SemaphoreType.DMA((3,)),
        ],
        compiler_params=pltpu.CompilerParams(
            collective_id=0, has_side_effects=True, vmem_limit_bytes=60 * 1024 * 1024
        ),
        name="attend",
    )(
        queries,
        new_keys.reshape(-1, width),
        new_values.reshape(-1, width),
        suffix_keys.reshape(requests, suffix * key_heads, width),
        suffix_values.reshape(requests, suffix * key_heads, width),
        suffix_len,
        prefix_keys.reshape(-1, width),
        prefix_values.reshape(-1, width),
        block_ids,
        block_lists.T,
    )


def solution(mesh):
    lead = ("groups", "loop")
    in_specs = (
        P(lead, None, None, None),
        P(lead, None, None, None),
        P(lead, None, None, None),
        P(lead, None, None, None),
        P(lead, None, None, None),
        P(lead),
        P(lead, None, None, None),
        P(lead, None, None, None),
        P(lead),
        P(lead, None),
    )
    return jax.shard_map(
        functools.partial(per_device, mesh.shape["loop"]),
        mesh=mesh,
        in_specs=in_specs,
        out_specs=P(lead, None, None, None),
        check_vma=False,
    )
```
